256 devices in a mesh: dp: 32 (over z_hi, y, core), mp: 8 (over x, z_lo).
Axes of the slice: x: 4, y: 4, z: 8 (z_hi: 4, z_lo: 2; z = z_hi * 2 + z_lo), core: 2. Of those that a mesh axis runs over, the one named last changes fastest.
Arguments:
- inputs: bfloat16 [12288, 6144], P('dp', 'mp'), may hold values from -16 to 16
- hidden_pre: bfloat16 [12288, 12288], P('dp', 'mp'), may hold values from -6 to 6
- hidden_grad: bfloat16 [12288, 12288], P('dp', 'mp'), may hold values from -16 to 16
- omega_in: bfloat16 [6144, 256], P('mp'), may hold values from -0.078125 to 0.078125
- omega_hid: bfloat16 [12288, 256], P('mp'), may hold values from -0.0546875 to 0.0546875
- owner_table: int32 [32, 1], replicated, may hold values from 0 to 1, as said below
Outputs:
- grad_pre: bfloat16 [6144, 12288], P('dp', 'mp')
- held_core: float32 [32, 256, 256], P('dp')
The draws below stay inside these ranges and needn't reach their ends.
Inputs may be any that keep to these rules, and one draw needn't show every extreme that they name: `owner_table`: each row names one factor, 0 for the input side and 1 for the hidden side; rows 0 and 2 name the same factor and row 1 the other.
All inputs are finite; a program needn't handle non-finite values.
Results may differ from the reference program's by a relative error of at most 0.035.
Values may be sent and summed in bfloat16 or wider, within the bound.
No kernel may reach another device: no remote copies, remote signals or barrier semaphores. Data moves between devices by JAX's collectives and lax.ppermute only.
A program may use at most 128 MiB of HBM per device.

```python
import jax
import jax.numpy as jnp
from jax import lax

D = 6144
FW = 12288
R = 256
TOK_DEV = 384
TOKENS = 12288
GROUPS = 32
N_DP = 32


def column_scales(scale_key, columns):
    return jnp.exp(jax.random.uniform(scale_key, (1, columns), jnp.float32, -1.15, 1.15))


def draw_inputs(key, part):
    key = jax.random.fold_in(key, 11)
    scale_key, entry_key = jax.random.split(key, 2)
    scales = column_scales(scale_key, D)
    entries = jnp.clip(jax.random.normal(entry_key, (TOKENS, D), jnp.float32), -5.0, 5.0)
    return (entries * scales).astype(jnp.bfloat16)


def draw_hidden_grad(key, part):
    key = jax.random.fold_in(key, 23)
    scale_key, entry_key = jax.random.split(key, 2)
    scales = column_scales(scale_key, FW)
    entries = jnp.clip(jax.random.normal(entry_key, (TOKENS, FW), jnp.float32), -5.0, 5.0)
    return (entries * scales).astype(jnp.bfloat16)


def draw_owner_table(key, part):
    key = jax.random.fold_in(key, 37)
    lead_key, rest_key = jax.random.split(key, 2)
    leading = jax.random.randint(lead_key, (), 0, 2, jnp.int32)
    drawn = jax.random.randint(rest_key, (GROUPS,), 0, 2, jnp.int32)
    places = jnp.arange(GROUPS, dtype=jnp.int32)
    fixed = jnp.where(places == 1, 1 - leading, leading)
    table = jnp.where(places < 3, fixed, drawn)
    return table[:, None].astype(jnp.int32)


def levels(rng, extent, pieces, low, largest):
    level, own = 1.0, jax.random.fold_in(rng, 6)
    for dim, parts in pieces:
        steps = jnp.exp(jax.random.uniform(jax.random.fold_in(own, dim), (parts,), jnp.float32, low / len(pieces), largest / len(pieces)))
        level = level * jnp.repeat(steps, extent[dim] // parts).reshape([-1 if axis == dim else 1 for axis in range(len(extent))])
    return level


def centred(key, shape, width, bound, pieces=(), kind=jnp.bfloat16):
    loudness = levels(key, shape, pieces, -0.22, 0.18) if pieces else 1.0
    array = jax.random.normal(key, shape, jnp.float32) * width * loudness
    return jnp.minimum(jnp.maximum(array, -bound), bound).astype(kind)


def setup_inputs(seed: int = 0) -> dict:
    key_of = jax.random.split(jax.random.key(seed), 7)
    return {
        "inputs": draw_inputs(jax.random.fold_in(key_of[6], 71), 0),
        "hidden_pre": centred(key_of[1], (TOKENS, FW), 1.0, 6.0, ((0, 32), (1, 8))),
        "hidden_grad": draw_hidden_grad(jax.random.fold_in(key_of[6], 71), 0),
        "omega_in": centred(key_of[3], (D, R), D ** -0.5, 0.078125, ((0, 8),)),
        "omega_hid": centred(key_of[4], (FW, R), FW ** -0.5, 0.0546875, ((0, 8),)),
        "owner_table": draw_owner_table(jax.random.fold_in(key_of[6], 71), 0),
    }


damping = 0.25
half_root = 0.7071067811865476
inverse_root_tau = 0.3989422804014327

def gelu_slope(pre_values):
    values = pre_values.astype(jnp.float32)
    return 0.5 * (1.0 + lax.erf(values * half_root)) + values * jnp.exp(-0.5 * values * values) * inverse_root_tau

def token_product(left_side, right_side):
    return lax.dot_general(left_side.astype(jnp.float32), right_side.astype(jnp.float32), (((0,), (0,)), ((), ())), preferred_element_type=jnp.float32)

def row_product(left_side, right_side):
    return lax.dot_general(left_side.astype(jnp.float32), right_side.astype(jnp.float32), (((1,), (1,)), ((), ())), preferred_element_type=jnp.float32)

def core_terms(sketch_basis, test_matrix):
    moment = jnp.dot(sketch_basis, test_matrix.astype(jnp.float32), precision=lax.Precision.HIGHEST)
    return damping * 0.5 * (moment + moment.T) + jnp.dot(sketch_basis, sketch_basis.T, precision=lax.Precision.HIGHEST)

def precondition(values, basis_low, reached, factor):
    solved = jax.scipy.linalg.cho_solve((factor, True), reached.T).T.astype(jnp.bfloat16)
    removed = jnp.dot(solved.astype(jnp.float32), basis_low.astype(jnp.float32), preferred_element_type=jnp.float32)
    return ((values.astype(jnp.float32) - removed) / damping).astype(jnp.bfloat16)

def reference(inputs, hidden_pre, hidden_grad, omega_in, omega_hid, owner_table):
    token_count = inputs.shape[0]
    hidden_err = (hidden_grad.astype(jnp.float32) * gelu_slope(hidden_pre)).astype(jnp.bfloat16)
    rows_in = jnp.dot(inputs.astype(jnp.float32), omega_in.astype(jnp.float32), preferred_element_type=jnp.float32).astype(jnp.bfloat16)
    rows_hid = jnp.dot(hidden_err.astype(jnp.float32), omega_hid.astype(jnp.float32), preferred_element_type=jnp.float32).astype(jnp.bfloat16)
    sketch_in = token_product(rows_in, inputs) / token_count
    sketch_hid = token_product(rows_hid, hidden_err) / token_count
    core_in = jnp.linalg.cholesky(core_terms(sketch_in, omega_in))
    core_hid = jnp.linalg.cholesky(core_terms(sketch_hid, omega_hid))
    held_core = jnp.where((owner_table[:, 0] == 0)[:, None, None], core_in[None], core_hid[None])
    low_in = sketch_in.astype(jnp.bfloat16)
    low_hid = sketch_hid.astype(jnp.bfloat16)
    hat_in = precondition(inputs, low_in, row_product(inputs, low_in), core_in)
    hat_hid = precondition(hidden_err, low_hid, row_product(hidden_err, low_hid), core_hid)

    def add_block(position, total):
        first_row = (position * TOK_DEV).astype(jnp.int32)
        left_side = lax.dynamic_slice_in_dim(hat_in, first_row, TOK_DEV, 0).astype(jnp.float32)
        right_side = lax.dynamic_slice_in_dim(hat_hid, first_row, TOK_DEV, 0).astype(jnp.float32)
        term = jnp.dot(left_side.T, right_side, precision=lax.Precision.HIGHEST) / token_count
        rounded = lax.optimization_barrier(term.astype(jnp.bfloat16))
        return total + rounded.astype(jnp.float32)
    total = lax.fori_loop(0, N_DP, add_block, jnp.zeros((D, FW), jnp.float32))
    return (total.astype(jnp.bfloat16), held_core)
```

```python
import functools

import jax
import jax.numpy as jnp
from jax import lax
from jax.experimental import pallas as pl
from jax.experimental.pallas import tpu as pltpu
from jax.sharding import Mesh
from jax.sharding import PartitionSpec as P

damping = 0.25
half_root = 0.7071067811865476
inverse_root_tau = 0.3989422804014327

PARTS = (("zh", 4), ("y", 4), ("c", 2), ("x", 4), ("zl", 2))
DP = ("zh", "y", "c")
MP = ("x", "zl")
N_DP = 32
N_MP = 8
PANEL = 64
GROUP = 8
bf16 = jnp.bfloat16
f32 = jnp.float32


def gelu_slope(pre_values):
    values = pre_values.astype(f32)
    return (
        0.5 * (1.0 + lax.erf(values * half_root))
        + values * jnp.exp(-0.5 * values * values) * inverse_root_tau
    )


def token_product(left_side, right_side):
    return lax.dot_general(
        left_side, right_side, (((0,), (0,)), ((), ())), preferred_element_type=f32
    )


def row_product(left_side, right_side):
    return lax.dot_general(
        left_side, right_side, (((1,), (1,)), ((), ())), preferred_element_type=f32
    )


def exact_dot(left_side, right_side, dims):
    return lax.dot_general(
        left_side,
        right_side,
        (dims, ((), ())),
        precision=lax.Precision.HIGHEST,
        preferred_element_type=f32,
    )


def exchange(parts, axis):
    return lax.all_to_all(parts, axis, 0, 0)


def sum_scatter(parts, axis):
    return exchange(parts, axis).astype(f32).sum(0).astype(bf16)


def collect(part, axis, count):
    return exchange(jnp.broadcast_to(part[None], (count,) + part.shape), axis)


def shift(value, axis, count, step):
    return lax.ppermute(value, axis, [(i, (i + step) % count) for i in range(count)])


def swap(value, axis):
    return lax.ppermute(value, axis, [(0, 1), (1, 0)])


def pick(stack, index):
    return lax.dynamic_index_in_dim(stack, index, 0, False)


def direct_collect(part, axis, count):
    me = lax.axis_index(axis)
    arrived = jnp.stack([part] + [shift(part, axis, count, k) for k in range(1, count)])
    return arrived[(me - jnp.arange(count)) % count]


def eliminate(block):
    size = block.shape[0]
    rows = lax.broadcasted_iota(jnp.int32, (size, size), 0)
    lanes = lax.broadcasted_iota(jnp.int32, (size, size), 1)
    work = jnp.concatenate([block, (lanes == rows).astype(f32)], axis=1)
    row_ids = lax.broadcasted_iota(jnp.int32, (size, 2 * size), 0)
    inverse_pivots = []
    for first in range(0, size, GROUP):
        columns = [
            jnp.broadcast_to(work[:, first + k : first + k + 1], (size, 2 * size))
            for k in range(GROUP)
        ]
        heads = [work[first + k : first + k + 1, :] for k in range(GROUP)]
        for k in range(GROUP):
            at = first + k
            inverse = 1.0 / columns[k][at : at + 1, :]
            inverse_pivots.append(inverse)
            factor = jnp.where(row_ids > at, columns[k] * inverse, 0.0)
            work = work - factor * heads[k]
            for later in range(k + 1, GROUP):
                columns[later] = columns[later] - factor * columns[later][at : at + 1, :]
                heads[later] = (
                    heads[later] - factor[first + later : first + later + 1, :] * heads[k]
                )
    return (work * jnp.sqrt(jnp.concatenate(inverse_pivots, axis=0)))[:, size:]


def factor_kernel(mats_ref, factor_ref, inverse_ref, work):
    count, size, _ = mats_ref.shape
    rows = lax.broadcasted_iota(jnp.int32, (size, size), 0)
    lanes = lax.broadcasted_iota(jnp.int32, (size, size), 1)
    for i in range(count):
        work[i, :, :size] = mats_ref[i]
        work[i, :, size:] = (rows == lanes).astype(f32)
    for low in range(0, size, PANEL):
        high = low + PANEL
        panels = []
        for i in range(count):
            small = eliminate(work[i, low:high, low:high])
            panel = exact_dot(small, work[i, low:high, :], ((1,), (0,)))
            work[i, low:high, :] = panel
            panels.append(panel)
        if high < size:
            for i in range(count):
                work[i, high:, :] = work[i, high:, :] - exact_dot(
                    panels[i][:, high:size], panels[i], ((0,), (0,))
                )
    for i in range(count):
        factor_ref[i] = jnp.where(rows <= lanes, work[i, :, :size], 0.0).T
        inverse_ref[i] = work[i, :, size:]


def factor_and_inverse(mats):
    count, size, _ = mats.shape
    return pl.pallas_call(
        factor_kernel,
        out_shape=[jax.ShapeDtypeStruct((count, size, size), f32)] * 2,
        in_specs=[pl.BlockSpec(memory_space=pltpu.VMEM)],
        out_specs=[pl.BlockSpec(memory_space=pltpu.VMEM)] * 2,
        scratch_shapes=[pltpu.VMEM((count, size, 2 * size), f32)],
        compiler_params=pltpu.CompilerParams(vmem_limit_bytes=16 * 2**20),
        cost_estimate=pl.CostEstimate(
            flops=6 * count * size**3, bytes_accessed=60_000_000, transcendentals=0
        ),
        name="factor_and_inverse",
    )(mats)


def core_terms(sketch_basis, test_matrix):
    moment = jnp.dot(sketch_basis, test_matrix.astype(f32), precision=lax.Precision.HIGHEST)
    return damping * 0.5 * (moment + moment.T) + jnp.dot(
        sketch_basis, sketch_basis.T, precision=lax.Precision.HIGHEST
    )


def two_halves(value):
    high = lax.reduce_precision(value, 8, 7)
    return jnp.concatenate([high.astype(bf16), (value - high).astype(bf16)], axis=-1)


def whole_value(halves):
    size = halves.shape[-1] // 2
    return halves[..., :size].astype(f32) + halves[..., size:].astype(f32)


def sum_over_dp(value):
    rows, width = value.shape
    me = lax.axis_index("c")
    halves = value.reshape(2, rows // 2, width)
    mine = pick(halves, me).astype(f32) + swap(pick(halves, 1 - me), "c").astype(f32)
    mine = mine.astype(bf16)
    part = sum_scatter(mine.reshape(4, rows // 8, width), "y")
    part = sum_scatter(part.reshape(4, rows // 32, width), "zh")
    part = collect(part, "zh", 4).reshape(rows // 8, width)
    part = collect(part, "y", 4).reshape(rows // 2, width)
    other = swap(part, "c")
    return jnp.where(
        me == 0, jnp.concatenate([part, other]), jnp.concatenate([other, part])
    )


def removed(values, solved, basis_low):
    taken = jnp.dot(solved, basis_low, preferred_element_type=f32)
    return ((values.astype(f32) - taken) / damping).astype(bf16)


def on_device(inputs, hidden_pre, hidden_grad, omega_in, omega_hid, owner_table):
    local_tokens, local_in = inputs.shape
    token_count = local_tokens * N_DP
    rank = omega_in.shape[1]
    block = local_in // 4
    iy, ic, izh, izl = (lax.axis_index(a) for a in ("y", "c", "zh", "zl"))

    hidden_err = (hidden_grad.astype(f32) * gelu_slope(hidden_pre)).astype(bf16)
    rows = jnp.concatenate(
        [
            jnp.dot(inputs, omega_in, preferred_element_type=f32).astype(bf16),
            jnp.dot(hidden_err, omega_hid, preferred_element_type=f32).astype(bf16),
        ],
        axis=1,
    )
    rows = sum_scatter(rows.reshape(N_MP, local_tokens // N_MP, 2 * rank), MP)
    rows = collect(rows, MP, N_MP).reshape(local_tokens, 2 * rank)

    hid_own = lax.all_gather(hidden_err, "y")
    hid_other = swap(hid_own, "c")
    hid_all = jnp.concatenate([hid_own, hid_other]).reshape(8 * local_tokens, -1)

    blocks = inputs.reshape(local_tokens, 2, 2, block)
    own_blocks = lax.dynamic_index_in_dim(blocks, ic, 2, False)
    for_other = lax.dynamic_index_in_dim(blocks, 1 - ic, 2, False)
    near = jnp.stack([own_blocks, swap(for_other, "c")])
    near = jnp.moveaxis(near, 2, 0)
    far = swap(near, "zl")
    by_zl = jnp.where(izl == 0, jnp.stack([near, far]), jnp.stack([far, near]))
    by_y = by_zl.reshape(4, 2, local_tokens, block)
    in_parts = [pick(by_y, iy)] + [
        shift(pick(by_y, (iy + k) % 4), "y", 4, k) for k in range(1, 4)
    ]
    in_parts = jnp.stack(in_parts)[(iy - jnp.arange(4)) % 4]
    in_parts = jnp.swapaxes(in_parts, 0, 1).reshape(8 * local_tokens, block)
    in_all = lax.all_gather(in_parts, "x")

    sketch = jnp.concatenate(
        [
            token_product(rows[:, :rank], inputs).astype(bf16),
            token_product(rows[:, rank:], hidden_err).astype(bf16),
        ],
        axis=1,
    )
    sketch = sum_over_dp(sketch).astype(f32) / token_count
    sketch_in, sketch_hid = sketch[:, :local_in], sketch[:, local_in:]
    low_in, low_hid = sketch_in.astype(bf16), sketch_hid.astype(bf16)

    low_block = pick(jnp.moveaxis(low_in.reshape(rank, 4, block), 1, 0), (iy % 2) * 2 + ic)
    low_block = jnp.where(izl == iy // 2, low_block, swap(low_block, "zl"))
    low_all = direct_collect(low_block, "x", 4)

    core = jnp.stack([core_terms(sketch_in, omega_in), core_terms(sketch_hid, omega_hid)])
    reach = jnp.concatenate(
        [row_product(inputs, low_in).astype(bf16), row_product(hidden_err, low_hid).astype(bf16)],
        axis=1,
    )
    core_rows = 2 * rank // N_MP
    both = jnp.concatenate(
        [
            two_halves(core.reshape(N_MP, core_rows, rank)),
            reach.reshape(N_MP, local_tokens // N_MP, 2 * rank),
        ],
        axis=1,
    )
    both = exchange(both, MP)
    core = whole_value(both[:, :core_rows]).sum(0)
    reach = both[:, core_rows:].astype(f32).sum(0).astype(bf16)
    both = collect(jnp.concatenate([two_halves(core), reach]), MP, N_MP)
    core = whole_value(both[:, :core_rows]).reshape(2, rank, rank)
    reach = both[:, core_rows:].reshape(local_tokens, 2 * rank)

    reach_own = direct_collect(reach, "y", 4)
    reach_all = jnp.concatenate([reach_own, swap(reach_own, "c")])
    reach_all = reach_all.reshape(8 * local_tokens, 2 * rank).astype(f32)

    core_factor, inverse = factor_and_inverse(core)
    owner = owner_table[lax.axis_index(DP), 0]
    held = jnp.where(owner == 0, core_factor[0], core_factor[1])[None]

    solved_in, solved_hid = (
        exact_dot(
            reach_all[:, i * rank : (i + 1) * rank],
            exact_dot(inverse[i], inverse[i], ((0,), (0,))),
            ((1,), (0,)),
        ).astype(bf16)
        for i in range(2)
    )
    half = hid_all.shape[1] // 2
    hat_hid = [
        removed(hid_all[:, i * half : (i + 1) * half], solved_hid, low_hid[:, i * half : (i + 1) * half])
        for i in range(2)
    ]

    def term(index, side):
        hat_in = removed(pick(in_all, index % 4), solved_in, pick(low_all, index % 4))
        return token_product(hat_in, hat_hid[side]) / token_count

    up = term(izh + 3, 0).astype(bf16)
    down = term(izh + 1, 1).astype(bf16)
    for step in range(1, 4):
        up = shift(up, "zh", 4, 1)
        down = shift(down, "zh", 4, 3)
        up = (up.astype(f32) + term(izh + 3 - step, 0)).astype(bf16)
        down = (down.astype(f32) + term(izh + 1 + step, 1)).astype(bf16)
    return (jnp.concatenate([up, down], axis=1), held)


def solution(mesh):
    parts = Mesh(
        mesh.devices.reshape([size for _, size in PARTS]), [name for name, _ in PARTS]
    )
    return jax.shard_map(
        on_device,
        mesh=parts,
        in_specs=(P(DP, MP), P(DP, MP), P(DP, MP), P(MP, None), P(MP, None), P()),
        out_specs=(P(DP, MP), P(DP, None, None)),
        check_vma=False,
    )
```

```python
import functools

import jax
import jax.numpy as jnp
from jax import lax
from jax.experimental import pallas as pl
from jax.experimental.pallas import tpu as pltpu
from jax.sharding import Mesh
from jax.sharding import PartitionSpec as P

damping = 0.25
half_root = 0.7071067811865476
inverse_root_tau = 0.3989422804014327

PARTS = (("zh", 4), ("y", 4), ("c", 2), ("x", 4), ("zl", 2))
DP = ("zh", "y", "c")
MP = ("x", "zl")
N_DP = 32
N_MP = 8
PANEL = 64
GROUP = 16
bf16 = jnp.bfloat16
f32 = jnp.float32


def gelu_slope(pre_values):
    values = pre_values.astype(f32)
    return (
        0.5 * (1.0 + lax.erf(values * half_root))
        + values * jnp.exp(-0.5 * values * values) * inverse_root_tau
    )


def token_product(left_side, right_side):
    return lax.dot_general(
        left_side, right_side, (((0,), (0,)), ((), ())), preferred_element_type=f32
    )


def row_product(left_side, right_side):
    return lax.dot_general(
        left_side, right_side, (((1,), (1,)), ((), ())), preferred_element_type=f32
    )


def exact_dot(left_side, right_side, dims):
    return lax.dot_general(
        left_side,
        right_side,
        (dims, ((), ())),
        precision=lax.Precision.HIGHEST,
        preferred_element_type=f32,
    )


def exchange(parts, axis):
    return lax.all_to_all(parts, axis, 0, 0)


def sum_scatter(parts, axis):
    return exchange(parts, axis).astype(f32).sum(0).astype(bf16)


def collect(part, axis, count):
    return exchange(jnp.broadcast_to(part[None], (count,) + part.shape), axis)


def shift(value, axis, count, step):
    return lax.ppermute(value, axis, [(i, (i + step) % count) for i in range(count)])


def swap(value, axis):
    return lax.ppermute(value, axis, [(0, 1), (1, 0)])


def pick(stack, index):
    return lax.dynamic_index_in_dim(stack, index, 0, False)


def after(value, *others):
    return lax.optimization_barrier((value,) + others)[0]


def line_up(parts, axis, pieces):
    count = len(parts)
    rows, columns = parts[0].shape[1:]
    if pieces == 1:
        shape = (count, rows, columns)
    else:
        shape = (rows, pieces * count * columns)

    def kernel(*refs):
        part_refs, out_ref, sems = refs[:count], refs[count], refs[count + 1]
        me = lax.axis_index(axis)
        copies = []
        for k in range(count):
            at = lax.rem(me - k + count, count)
            for piece in range(pieces):
                if pieces == 1:
                    target = out_ref.at[at]
                else:
                    start = pl.multiple_of((piece * count + at) * columns, columns)
                    target = out_ref.at[:, pl.ds(start, columns)]
                copies.append(
                    pltpu.make_async_copy(
                        part_refs[k].at[piece], target, sems.at[k * pieces + piece]
                    )
                )
        for copy in copies:
            copy.start()
        for copy in copies:
            copy.wait()

    return pl.pallas_call(
        kernel,
        out_shape=jax.ShapeDtypeStruct(shape, parts[0].dtype),
        in_specs=[pl.BlockSpec(memory_space=pl.ANY)] * count,
        out_specs=pl.BlockSpec(memory_space=pltpu.HBM),
        scratch_shapes=[pltpu.SemaphoreType.DMA((count * pieces,))],
        compiler_params=pltpu.CompilerParams(vmem_limit_bytes=2**20),
        name="line_up",
    )(*parts)


def eliminate(block):
    size = block.shape[0]
    rows = lax.broadcasted_iota(jnp.int32, (size, size), 0)
    lanes = lax.broadcasted_iota(jnp.int32, (size, size), 1)
    work = jnp.concatenate([block, (lanes == rows).astype(f32)], axis=1)
    row_ids = lax.broadcasted_iota(jnp.int32, (size, 2 * size), 0)
    inverse_pivots = []
    for first in range(0, size, GROUP):
        columns = [
            jnp.broadcast_to(work[:, first + k : first + k + 1], (size, 2 * size))
            for k in range(GROUP)
        ]
        heads = [work[first + k : first + k + 1, :] for k in range(GROUP)]
        for k in range(GROUP):
            at = first + k
            inverse = 1.0 / columns[k][at : at + 1, :]
            inverse_pivots.append(inverse)
            factor = jnp.where(row_ids > at, columns[k] * inverse, 0.0)
            work = work - factor * heads[k]
            for later in range(k + 1, GROUP):
                columns[later] = columns[later] - factor * columns[later][at : at + 1, :]
                heads[later] = (
                    heads[later] - factor[first + later : first + later + 1, :] * heads[k]
                )
    return (work * jnp.sqrt(jnp.concatenate(inverse_pivots, axis=0)))[:, size:]


def factor_kernel(owner_ref, both_ref, held_ref, inverse_ref, work):
    count, size, _ = inverse_ref.shape
    pieces = both_ref.shape[0] // count
    piece = size // pieces
    rows = lax.broadcasted_iota(jnp.int32, (size, size), 0)
    lanes = lax.broadcasted_iota(jnp.int32, (size, size), 1)
    for i in range(count):
        for k in range(pieces):
            halves = both_ref[i * pieces + k, :piece, :].astype(f32)
            work[i, k * piece : (k + 1) * piece, :size] = halves[:, :size] + halves[:, size:]
        work[i, :, size:] = (rows == lanes).astype(f32)
    for low in range(0, size, PANEL):
        high = low + PANEL
        panels = []
        for i in range(count):
            small = eliminate(work[i, low:high, low:high])
            panel = exact_dot(small, work[i, low:high, :], ((1,), (0,)))
            work[i, low:high, :] = panel
            panels.append(panel)
        if high < size:
            for i in range(count):
                work[i, high:, :] = work[i, high:, :] - exact_dot(
                    panels[i][:, high:size], panels[i], ((0,), (0,))
                )
    for i in range(count):
        @pl.when(owner_ref[0] == i)
        def _(i=i):
            held_ref[0] = jnp.where(rows <= lanes, work[i, :, :size], 0.0).T

        inverse_ref[i] = exact_dot(work[i, :, size:], work[i, :, size:], ((0,), (0,)))


def factor_and_inverse(owner, both, size):
    return pl.pallas_call(
        factor_kernel,
        out_shape=[
            jax.ShapeDtypeStruct((1, size, size), f32),
            jax.ShapeDtypeStruct((2, size, size), f32),
        ],
        in_specs=[
            pl.BlockSpec(memory_space=pltpu.SMEM),
            pl.BlockSpec(memory_space=pltpu.VMEM),
        ],
        out_specs=[pl.BlockSpec(memory_space=pltpu.VMEM)] * 2,
        scratch_shapes=[pltpu.VMEM((2, size, 2 * size), f32)],
        compiler_params=pltpu.CompilerParams(vmem_limit_bytes=16 * 2**20),
        cost_estimate=pl.CostEstimate(
            flops=12 * size**3, bytes_accessed=60_000_000, transcendentals=0
        ),
        name="factor_and_inverse",
    )(owner, both)


def solve_kernel(*refs):
    reach_refs, low_refs, inverse_ref, out_ref, low_ref = refs[:4], refs[4:8], *refs[8:]
    size = inverse_ref.shape[1]
    iy, ix = lax.axis_index("y"), lax.axis_index("x")
    inverses = []
    for i in range(2):
        rest, pieces = inverse_ref[i], []
        for _ in range(3):
            pieces.append(rest.astype(bf16))
            rest = rest - pieces[-1].astype(f32)
        inverses.append(pieces)
    for k in range(4):
        low_ref[lax.rem(ix - k + 4, 4)] = low_refs[k][...]
        at = lax.rem(iy - k + 4, 4)
        for i in range(2):
            reach = reach_refs[k][:, i * size : (i + 1) * size]
            solved = sum(
                jnp.dot(reach, piece, preferred_element_type=f32) for piece in inverses[i][::-1]
            )
            out_ref[at, :, i * size : (i + 1) * size] = solved.astype(bf16)


def solve(reach_parts, low_parts, inverse):
    return pl.pallas_call(
        solve_kernel,
        out_shape=[
            jax.ShapeDtypeStruct((4,) + reach_parts[0].shape, bf16),
            jax.ShapeDtypeStruct((4,) + low_parts[0].shape, bf16),
        ],
        in_specs=[pl.BlockSpec(memory_space=pltpu.VMEM)] * 9,
        out_specs=[pl.BlockSpec(memory_space=pltpu.VMEM)] * 2,
        compiler_params=pltpu.CompilerParams(vmem_limit_bytes=16 * 2**20),
        name="solve",
    )(*reach_parts, *low_parts, inverse)


def removed(values, taken):
    return ((values.astype(f32) - taken) / damping).astype(bf16)


def add_term(total, term, step):
    @pl.when(step == 0)
    def _():
        total[...] = term

    @pl.when(step > 0)
    def _():
        total[...] = total[...] + term


def first_kernel(
    token_count, own_ref, other_ref, in_ref, solved_own_ref, solved_other_ref, low_in_ref, low_hid_ref,
    hat_ref, up_ref, down_ref, up_total, down_total
):
    step, steps = pl.program_id(0), pl.num_programs(0)
    me = lax.axis_index("zh")
    rank, columns = low_hid_ref.shape
    own = step < steps // 2
    hidden = jnp.where(own, own_ref[...], other_ref[...])
    solved = jnp.where(own, solved_own_ref[...], solved_other_ref[...])
    hat_hid = removed(
        hidden, jnp.dot(solved[:, rank:], low_hid_ref[...], preferred_element_type=f32)
    )
    hat_ref[...] = hat_hid
    for total, off, start in ((up_total, 3, 0), (down_total, 1, columns // 2)):
        at = lax.rem(me + off, 4)
        hat_in = removed(in_ref[at], row_product(low_in_ref[at], solved[:, :rank]))
        part = hat_hid[:, start : start + columns // 2]
        add_term(total, jnp.dot(hat_in, part, preferred_element_type=f32), step)

    @pl.when(step == steps - 1)
    def _():
        up_ref[...] = (up_total[...] / token_count).astype(bf16)
        down_ref[...] = (down_total[...] / token_count).astype(bf16)


def rest_kernel(
    token_count, hat_ref, in_ref, solved_own_ref, solved_other_ref, low_in_ref, up_ref, down_ref, hat_in, up_total, down_total
):
    step, steps = pl.program_id(0), pl.num_programs(0)
    me = lax.axis_index("zh")
    rank, columns = low_in_ref.shape[2], hat_ref.shape[1]
    rows = in_ref.shape[1]
    own = step < steps // 2
    solved = jnp.where(own, solved_own_ref[...], solved_other_ref[...])[:, :rank]
    for k, off in enumerate((1, 0, 2, 3)):
        at = lax.rem(me + off, 4)
        hat_in[k * rows : (k + 1) * rows, :] = removed(in_ref[at], row_product(low_in_ref[at], solved))
    for total, low, start in ((up_total, 0, 0), (down_total, rows, columns // 2)):
        term = jnp.dot(
            hat_in[low : low + 3 * rows, :],
            hat_ref[:, start : start + columns // 2],
            preferred_element_type=f32,
        )
        add_term(total, term, step)

    @pl.when(step == steps - 1)
    def _():
        up_ref[...] = (up_total[...] / token_count).astype(bf16)
        down_ref[...] = (down_total[...] / token_count).astype(bf16)


def gradient(hid_own, hid_other, in_all, solved_own, solved_other, low_in, low_hid, token_count):
    tokens, columns = hid_own.shape
    parts, rows, _ = in_all.shape
    rank = low_hid.shape[0]
    chunk, half = tokens // 2, columns // 2

    def first(i):
        return jnp.minimum(i, 1), 0

    def second(i):
        return jnp.maximum(i - 2, 0), 0

    solved_specs = [
        pl.BlockSpec((chunk, 2 * rank), first),
        pl.BlockSpec((chunk, 2 * rank), second),
        pl.BlockSpec((parts, rows, rank), lambda i: (0, 0, 0)),
    ]
    in_spec = pl.BlockSpec((parts, rows, chunk), lambda i: (0, 0, i))
    hat_spec = pl.BlockSpec((chunk, columns), lambda i: (i, 0))
    hat_hid, up, down = pl.pallas_call(
        functools.partial(first_kernel, token_count),
        out_shape=[
            jax.ShapeDtypeStruct((2 * tokens, columns), bf16),
            jax.ShapeDtypeStruct((rows, half), bf16),
            jax.ShapeDtypeStruct((rows, half), bf16),
        ],
        grid=(4,),
        in_specs=[
            pl.BlockSpec((chunk, columns), first),
            pl.BlockSpec((chunk, columns), second),
            in_spec,
            *solved_specs,
            pl.BlockSpec((rank, columns), lambda i: (0, 0)),
        ],
        out_specs=[hat_spec] + [pl.BlockSpec((rows, half), lambda i: (0, 0))] * 2,
        scratch_shapes=[pltpu.VMEM((rows, half), f32)] * 2,
        compiler_params=pltpu.CompilerParams(vmem_limit_bytes=48 * 2**20),
        cost_estimate=pl.CostEstimate(
            flops=5_000_000_000, bytes_accessed=20_000_000, transcendentals=0
        ),
        name="gradient_first",
    )(hid_own, hid_other, in_all, solved_own, solved_other, low_in, low_hid)
    more_up, more_down = pl.pallas_call(
        functools.partial(rest_kernel, token_count),
        out_shape=[jax.ShapeDtypeStruct((3 * rows, half), bf16)] * 2,
        grid=(4,),
        in_specs=[hat_spec, in_spec, *solved_specs],
        out_specs=[pl.BlockSpec((3 * rows, half), lambda i: (0, 0))] * 2,
        scratch_shapes=[pltpu.VMEM((4 * rows, chunk), bf16)]
        + [pltpu.VMEM((3 * rows, half), f32)] * 2,
        compiler_params=pltpu.CompilerParams(vmem_limit_bytes=48 * 2**20),
        cost_estimate=pl.CostEstimate(
            flops=7_000_000_000, bytes_accessed=20_000_000, transcendentals=0
        ),
        name="gradient_rest",
    )(hat_hid, in_all, solved_own, solved_other, low_in)
    return up, down, more_up, more_down


def project_kernel(
    token_count, mine_ref, other_ref, omega_in_ref, omega_hid_ref, in_ref, hid_ref, both_ref, low_ref, blocks_ref, sketch_ref
):
    rank = sketch_ref.shape[0]
    me = lax.axis_index("c")
    sketch_ref[pl.ds(pl.multiple_of(me * (rank // 2), rank // 2), rank // 2), :] = mine_ref[...]
    sketch_ref[pl.ds(pl.multiple_of((1 - me) * (rank // 2), rank // 2), rank // 2), :] = other_ref[...]
    pieces = both_ref.shape[0]
    core_rows = 2 * rank // pieces
    tokens = in_ref.shape[0] // pieces
    start = 0
    for i, (omega, values) in enumerate(((omega_in_ref, in_ref), (omega_hid_ref, hid_ref))):
        end = start + values.shape[1]
        basis = sketch_ref[:, start:end]
        moment = jnp.dot(basis, omega[...], preferred_element_type=f32) / token_count
        square = row_product(basis, basis) / (float(token_count) * token_count)
        core = damping * 0.5 * (moment + moment.T) + square
        high = core.astype(bf16)
        rest = (core - high.astype(f32)).astype(bf16)
        low = (basis.astype(f32) / token_count).astype(bf16)
        if i == 0:
            turned = low.astype(f32).T.astype(bf16)
            block = blocks_ref.shape[1]
            for k in range(blocks_ref.shape[0]):
                blocks_ref[k] = turned[k * block : (k + 1) * block]
        else:
            low_ref[...] = low
        reach = row_product(values[...], low).astype(bf16)
        for k in range(pieces // 2):
            at = slice(k * core_rows, (k + 1) * core_rows)
            both_ref[i * pieces // 2 + k, :core_rows, :rank] = high[at]
            both_ref[i * pieces // 2 + k, :core_rows, rank:] = rest[at]
        for k in range(pieces):
            both_ref[k, core_rows:, i * rank : (i + 1) * rank] = reach[k * tokens : (k + 1) * tokens]
        start = end


def project(mine, other, omega_in, omega_hid, inputs, hidden_err, token_count):
    rank, width = 2 * mine.shape[0], mine.shape[1]
    tokens, local_in = inputs.shape
    rows = 2 * rank // N_MP + tokens // N_MP
    return pl.pallas_call(
        functools.partial(project_kernel, token_count),
        out_shape=[
            jax.ShapeDtypeStruct((N_MP, rows, 2 * rank), bf16),
            jax.ShapeDtypeStruct((rank, width - local_in), bf16),
            jax.ShapeDtypeStruct((4, local_in // 4, rank), bf16),
        ],
        in_specs=[pl.BlockSpec(memory_space=pltpu.VMEM)] * 6,
        out_specs=[pl.BlockSpec(memory_space=pltpu.VMEM)] * 3,
        scratch_shapes=[pltpu.VMEM((rank, width), bf16)],
        compiler_params=pltpu.CompilerParams(vmem_limit_bytes=24 * 2**20),
        name="project",
    )(mine, other, omega_in, omega_hid, inputs, hidden_err)


def two_halves(value):
    high = lax.reduce_precision(value, 8, 7)
    return jnp.concatenate([high.astype(bf16), (value - high).astype(bf16)], axis=-1)


def whole_value(halves):
    size = halves.shape[-1] // 2
    return halves[..., :size].astype(f32) + halves[..., size:].astype(f32)


def on_device(inputs, hidden_pre, hidden_grad, omega_in, omega_hid, owner_table):
    local_tokens, local_in = inputs.shape
    token_count = local_tokens * N_DP
    rank = omega_in.shape[1]
    block = local_in // 4
    near_tokens = 4 * local_tokens
    iy, ic, izh, izl = (lax.axis_index(a) for a in ("y", "c", "zh", "zl"))

    far = swap(inputs, "zl")

    hidden_err = (hidden_grad.astype(f32) * gelu_slope(hidden_pre)).astype(bf16)
    rows = jnp.concatenate(
        [
            jnp.dot(inputs, omega_in, preferred_element_type=f32).astype(bf16),
            jnp.dot(hidden_err, omega_hid, preferred_element_type=f32).astype(bf16),
        ],
        axis=1,
    )
    rows = after(rows.reshape(N_MP, local_tokens // N_MP, 2 * rank), far)
    rows = sum_scatter(rows, MP)
    near, far = (v.T.reshape(2, 2, block, local_tokens) for v in (inputs, far))
    for_y = []
    for k in range(4):
        to = (iy + k) % 4
        for_y.append(jnp.where(izl == to // 2, pick(near, to % 2), pick(far, to % 2)))
    in_parts = [for_y[0]] + [shift(for_y[k], "y", 4, k) for k in range(1, 4)]
    rows, in_parts[1], in_parts[3] = lax.optimization_barrier((rows, in_parts[1], in_parts[3]))
    rows = collect(rows, MP, N_MP).reshape(local_tokens, 2 * rank)
    rows, in_parts[2] = lax.optimization_barrier((rows, in_parts[2]))
    in_parts = jnp.stack(in_parts)
    in_parts = jnp.stack([pick(jnp.moveaxis(in_parts, 1, 0), ic), swap(pick(jnp.moveaxis(in_parts, 1, 0), 1 - ic), "c")])
    in_parts = [in_parts[:, k] for k in range(4)]

    sketch = jnp.concatenate(
        [
            token_product(rows[:, :rank], inputs).astype(bf16),
            token_product(rows[:, rank:], hidden_err).astype(bf16),
        ],
        axis=1,
    )
    in_near = line_up(in_parts, "y", 2)
    in_all = lax.all_gather(in_near, "x")

    width = sketch.shape[1]
    halves = sketch.reshape(2, rank // 2, width)
    part = pick(halves, ic).astype(f32) + swap(pick(halves, 1 - ic), "c").astype(f32)
    part = after(part.astype(bf16), in_near)
    part = sum_scatter(part.reshape(4, rank // 8, width), "y")
    part = sum_scatter(part.reshape(4, rank // 32, width), "zh")
    hid_own = lax.all_gather(hidden_err, "y").reshape(near_tokens, -1)
    part = collect(part, "zh", 4).reshape(rank // 8, width)
    part = collect(part, "y", 4).reshape(rank // 2, width)
    other = swap(part, "c")
    both, low_hid, low_blocks = project(
        part, other, omega_in, omega_hid, inputs, hidden_err, token_count
    )
    low_block = pick(low_blocks, (iy % 2) * 2 + ic)
    low_far = swap(low_block, "zl")
    both = exchange(after(both, in_all), MP)
    both, low_far = lax.optimization_barrier((both, low_far))
    low_block = jnp.where(izl == iy // 2, low_block, low_far)
    low_parts = [low_block] + [shift(low_block, "x", 4, k) for k in range(1, 4)]
    core_rows = 2 * rank // N_MP
    core = whole_value(both[:, :core_rows]).sum(0)
    reach = both[:, core_rows:].astype(f32).sum(0).astype(bf16)
    both = jnp.concatenate([two_halves(core), reach])
    both = collect(both, MP, N_MP)
    reach = both[:, core_rows:].reshape(local_tokens, 2 * rank)

    reach_parts = [reach] + [shift(reach, "y", 4, k) for k in range(1, 4)]
    both, low_parts = lax.optimization_barrier((both, low_parts))
    hid_own = after(hid_own, both)
    hid_other = swap(hid_own, "c")
    owner = owner_table[lax.axis_index(DP)]
    held, inverse = factor_and_inverse(owner, both, rank)
    inverse, reach_parts = lax.optimization_barrier((inverse, reach_parts))
    solved_own, low_in = solve(reach_parts, low_parts, inverse)
    solved_own = solved_own.reshape(near_tokens, 2 * rank)
    solved_other = swap(solved_own, "c")
    up, down, more_up, more_down = gradient(
        hid_own, hid_other, in_all, solved_own, solved_other, low_in, low_hid, token_count
    )
    quarter = up.shape[1] // 2
    done = []
    for value, more, turn, order in ((up, more_up, 1, (2, 0, 1)), (down, more_down, 3, (1, 2, 0))):
        for k in range(2):
            columns = slice(k * quarter, (k + 1) * quarter)
            running = value[:, columns]
            for at in order:
                running = shift(running, "zh", 4, turn).astype(f32)
                here = more[at * block : (at + 1) * block, columns].astype(f32)
                running = (running + here).astype(bf16)
            done.append(running)
    return (jnp.concatenate(done, axis=1), held)


def solution(mesh):
    parts = Mesh(
        mesh.devices.reshape([size for _, size in PARTS]), [name for name, _ in PARTS]
    )
    return jax.shard_map(
        on_device,
        mesh=parts,
        in_specs=(P(DP, MP), P(DP, MP), P(DP, MP), P(MP, None), P(MP, None), P()),
        out_specs=(P(DP, MP), P(DP, None, None)),
        check_vma=False,
    )
```

```python
import functools

import jax
import jax.numpy as jnp
from jax import lax
from jax.experimental import pallas as pl
from jax.experimental.pallas import tpu as pltpu
from jax.sharding import Mesh
from jax.sharding import PartitionSpec as P

damping = 0.25
half_root = 0.7071067811865476
inverse_root_tau = 0.3989422804014327

PARTS = (("zh", 4), ("y", 4), ("c", 2), ("x", 4), ("zl", 2))
DP = ("zh", "y", "c")
MP = ("x", "zl")
N_DP = 32
N_MP = 8
PANEL = 64
GROUP = 16
bf16 = jnp.bfloat16
f32 = jnp.float32


def gelu_slope(pre_values):
    values = pre_values.astype(f32)
    return (
        0.5 * (1.0 + lax.erf(values * half_root))
        + values * jnp.exp(-0.5 * values * values) * inverse_root_tau
    )


def token_product(left_side, right_side):
    return lax.dot_general(
        left_side, right_side, (((0,), (0,)), ((), ())), preferred_element_type=f32
    )


def row_product(left_side, right_side):
    return lax.dot_general(
        left_side, right_side, (((1,), (1,)), ((), ())), preferred_element_type=f32
    )


def exact_dot(left_side, right_side, dims):
    return lax.dot_general(
        left_side,
        right_side,
        (dims, ((), ())),
        precision=lax.Precision.HIGHEST,
        preferred_element_type=f32,
    )


def exchange(parts, axis):
    return lax.all_to_all(parts, axis, 0, 0)


def sum_scatter(parts, axis):
    return exchange(parts, axis).astype(f32).sum(0).astype(bf16)


def collect(part, axis, count):
    return exchange(jnp.broadcast_to(part[None], (count,) + part.shape), axis)


def shift(value, axis, count, step):
    return lax.ppermute(value, axis, [(i, (i + step) % count) for i in range(count)])


def swap(value, axis):
    return lax.ppermute(value, axis, [(0, 1), (1, 0)])


def pick(stack, index):
    return lax.dynamic_index_in_dim(stack, index, 0, False)


def after(value, *others):
    return lax.optimization_barrier((value,) + others)[0]


def line_up(parts, axis, pieces):
    count = len(parts)
    rows, columns = parts[0].shape[1:]
    if pieces == 1:
        shape = (count, rows, columns)
    else:
        shape = (rows, pieces * count * columns)

    def kernel(*refs):
        part_refs, out_ref, sems = refs[:count], refs[count], refs[count + 1]
        me = lax.axis_index(axis)
        copies = []
        for k in range(count):
            at = lax.rem(me - k + count, count)
            for piece in range(pieces):
                if pieces == 1:
                    target = out_ref.at[at]
                else:
                    start = pl.multiple_of((piece * count + at) * columns, columns)
                    target = out_ref.at[:, pl.ds(start, columns)]
                copies.append(
                    pltpu.make_async_copy(
                        part_refs[k].at[piece], target, sems.at[k * pieces + piece]
                    )
                )
        for copy in copies:
            copy.start()
        for copy in copies:
            copy.wait()

    return pl.pallas_call(
        kernel,
        out_shape=jax.ShapeDtypeStruct(shape, parts[0].dtype),
        in_specs=[pl.BlockSpec(memory_space=pl.ANY)] * count,
        out_specs=pl.BlockSpec(memory_space=pltpu.HBM),
        scratch_shapes=[pltpu.SemaphoreType.DMA((count * pieces,))],
        compiler_params=pltpu.CompilerParams(vmem_limit_bytes=2**20),
        name="line_up",
    )(*parts)


def eliminate(block):
    size = block.shape[0]
    rows = lax.broadcasted_iota(jnp.int32, (size, size), 0)
    lanes = lax.broadcasted_iota(jnp.int32, (size, size), 1)
    work = jnp.concatenate([block, (lanes == rows).astype(f32)], axis=1)
    row_ids = lax.broadcasted_iota(jnp.int32, (size, 2 * size), 0)
    inverse_pivots = []
    for first in range(0, size, GROUP):
        columns = [
            jnp.broadcast_to(work[:, first + k : first + k + 1], (size, 2 * size))
            for k in range(GROUP)
        ]
        heads = [work[first + k : first + k + 1, :] for k in range(GROUP)]
        for k in range(GROUP):
            at = first + k
            inverse = 1.0 / columns[k][at : at + 1, :]
            inverse_pivots.append(inverse)
            factor = jnp.where(row_ids > at, columns[k] * inverse, 0.0)
            work = work - factor * heads[k]
            for later in range(k + 1, GROUP):
                columns[later] = columns[later] - factor * columns[later][at : at + 1, :]
                heads[later] = (
                    heads[later] - factor[first + later : first + later + 1, :] * heads[k]
                )
    return (work * jnp.sqrt(jnp.concatenate(inverse_pivots, axis=0)))[:, size:]


def factor_kernel(owner_ref, both_ref, held_ref, inverse_ref, work):
    count, size, _ = inverse_ref.shape
    pieces = both_ref.shape[0] // count
    piece = size // pieces
    rows = lax.broadcasted_iota(jnp.int32, (size, size), 0)
    lanes = lax.broadcasted_iota(jnp.int32, (size, size), 1)
    for i in range(count):
        for k in range(pieces):
            halves = both_ref[i * pieces + k, :piece, :].astype(f32)
            work[i, k * piece : (k + 1) * piece, :size] = halves[:, :size] + halves[:, size:]
        work[i, :, size:] = (rows == lanes).astype(f32)
    for low in range(0, size, PANEL):
        high = low + PANEL
        panels = []
        for i in range(count):
            small = eliminate(work[i, low:high, low:high])
            panel = exact_dot(small, work[i, low:high, :], ((1,), (0,)))
            work[i, low:high, :] = panel
            panels.append(panel)
        if high < size:
            for i in range(count):
                work[i, high:, :] = work[i, high:, :] - exact_dot(
                    panels[i][:, high:size], panels[i], ((0,), (0,))
                )
    for i in range(count):
        @pl.when(owner_ref[0] == i)
        def _(i=i):
            held_ref[0] = jnp.where(rows <= lanes, work[i, :, :size], 0.0).T

        inverse_ref[i] = exact_dot(work[i, :, size:], work[i, :, size:], ((0,), (0,)))


def factor_and_inverse(owner, both, size):
    return pl.pallas_call(
        factor_kernel,
        out_shape=[
            jax.ShapeDtypeStruct((1, size, size), f32),
            jax.ShapeDtypeStruct((2, size, size), f32),
        ],
        in_specs=[
            pl.BlockSpec(memory_space=pltpu.SMEM),
            pl.BlockSpec(memory_space=pltpu.VMEM),
        ],
        out_specs=[pl.BlockSpec(memory_space=pltpu.VMEM)] * 2,
        scratch_shapes=[pltpu.VMEM((2, size, 2 * size), f32)],
        compiler_params=pltpu.CompilerParams(vmem_limit_bytes=16 * 2**20),
        cost_estimate=pl.CostEstimate(
            flops=12 * size**3, bytes_accessed=60_000_000, transcendentals=0
        ),
        name="factor_and_inverse",
    )(owner, both)


def solve_kernel(*refs):
    reach_refs, low_refs, inverse_ref, out_ref, low_ref = refs[:4], refs[4:8], *refs[8:]
    size = inverse_ref.shape[1]
    iy, ix = lax.axis_index("y"), lax.axis_index("x")
    inverses = []
    for i in range(2):
        rest, pieces = inverse_ref[i], []
        for _ in range(3):
            pieces.append(rest.astype(bf16))
            rest = rest - pieces[-1].astype(f32)
        inverses.append(pieces)
    for k in range(4):
        low_ref[lax.rem(ix - k + 4, 4)] = low_refs[k][...]
        at = lax.rem(iy - k + 4, 4)
        for i in range(2):
            reach = reach_refs[k][:, i * size : (i + 1) * size]
            solved = sum(
                jnp.dot(reach, piece, preferred_element_type=f32) for piece in inverses[i][::-1]
            )
            out_ref[at, :, i * size : (i + 1) * size] = solved.astype(bf16)


def solve(reach_parts, low_parts, inverse):
    return pl.pallas_call(
        solve_kernel,
        out_shape=[
            jax.ShapeDtypeStruct((4,) + reach_parts[0].shape, bf16),
            jax.ShapeDtypeStruct((4,) + low_parts[0].shape, bf16),
        ],
        in_specs=[pl.BlockSpec(memory_space=pltpu.VMEM)] * 9,
        out_specs=[pl.BlockSpec(memory_space=pltpu.VMEM)] * 2,
        compiler_params=pltpu.CompilerParams(vmem_limit_bytes=16 * 2**20),
        name="solve",
    )(*reach_parts, *low_parts, inverse)


def removed(values, taken):
    return ((values.astype(f32) - taken) * (1.0 / damping)).astype(bf16)


def add_term(total, term, step):
    @pl.when(step == 0)
    def _():
        total[...] = term

    @pl.when(step > 0)
    def _():
        total[...] = total[...] + term


def first_kernel(scale, hidden_ref, in_ref, solved_ref, low_in_ref, low_hid_ref, *refs):
    before, (hat_ref, up_ref, down_ref, up_total, down_total) = refs[:-5], refs[-5:]
    step, steps = pl.program_id(0), pl.num_programs(0)
    me = lax.axis_index("zh")
    rank, columns = low_hid_ref.shape
    taken = jnp.dot(solved_ref[:, rank:], low_hid_ref[...], preferred_element_type=f32)
    hat_hid = removed(hidden_ref[...], taken)
    hat_ref[...] = hat_hid
    for total, off, start in ((up_total, 3, 0), (down_total, 1, columns // 2)):
        at = lax.rem(me + off, 4)
        hat_in = removed(in_ref[at], row_product(low_in_ref[at], solved_ref[:, :rank]))
        part = hat_hid[:, start : start + columns // 2]
        add_term(total, jnp.dot(hat_in, part, preferred_element_type=f32), step)

    @pl.when(step == steps - 1)
    def _():
        up, down = up_total[...], down_total[...]
        if before:
            up, down = up + before[0][...], down + before[1][...]
        up_ref[...] = (up * scale).astype(up_ref.dtype)
        down_ref[...] = (down * scale).astype(down_ref.dtype)


def rest_kernel(
    scale, hat_own_ref, hat_other_ref, in_ref, solved_own_ref, solved_other_ref, low_in_ref, up_ref, down_ref, hat_in, up_total, down_total
):
    step, steps = pl.program_id(0), pl.num_programs(0)
    me = lax.axis_index("zh")
    rank, columns = low_in_ref.shape[2], hat_own_ref.shape[1]
    rows = in_ref.shape[1]

    def body(hat_ref, solved_ref):
        for k, off in enumerate((1, 0, 2, 3)):
            at = lax.rem(me + off, 4)
            taken = row_product(low_in_ref[at], solved_ref[:, :rank])
            hat_in[k * rows : (k + 1) * rows, :] = removed(in_ref[at], taken)
        for total, low, start in ((up_total, 0, 0), (down_total, rows, columns // 2)):
            term = jnp.dot(
                hat_in[low : low + 3 * rows, :],
                hat_ref[:, start : start + columns // 2],
                preferred_element_type=f32,
            )
            add_term(total, term, step)

    pl.when(step < steps // 2)(functools.partial(body, hat_own_ref, solved_own_ref))
    pl.when(step >= steps // 2)(functools.partial(body, hat_other_ref, solved_other_ref))

    @pl.when(step == steps - 1)
    def _():
        up_ref[...] = (up_total[...] * scale).astype(bf16)
        down_ref[...] = (down_total[...] * scale).astype(bf16)


def gradient_first(core, hidden, in_all, solved, low_in, low_hid, before, token_count):
    tokens, columns = hidden.shape
    parts, rows, _ = in_all.shape
    rank = low_hid.shape[0]
    chunk, half = tokens // 2, columns // 2
    last = len(before) > 0
    block_spec = pl.BlockSpec((rows, half), lambda i: (0, 0))
    return pl.pallas_call(
        functools.partial(first_kernel, 1.0 / token_count if last else 1.0),
        out_shape=[
            jax.ShapeDtypeStruct((tokens, columns), bf16),
            jax.ShapeDtypeStruct((rows, half), bf16 if last else f32),
            jax.ShapeDtypeStruct((rows, half), bf16 if last else f32),
        ],
        grid=(2,),
        in_specs=[
            pl.BlockSpec((chunk, columns), lambda i: (i, 0)),
            pl.BlockSpec((parts, rows, chunk), lambda i: (0, 0, 2 * core + i)),
            pl.BlockSpec((chunk, 2 * rank), lambda i: (i, 0)),
            pl.BlockSpec((parts, rows, rank), lambda i: (0, 0, 0)),
            pl.BlockSpec((rank, columns), lambda i: (0, 0)),
        ]
        + [block_spec] * len(before),
        out_specs=[pl.BlockSpec((chunk, columns), lambda i: (i, 0)), block_spec, block_spec],
        scratch_shapes=[pltpu.VMEM((rows, half), f32)] * 2,
        compiler_params=pltpu.CompilerParams(vmem_limit_bytes=56 * 2**20),
        cost_estimate=pl.CostEstimate(
            flops=2_500_000_000, bytes_accessed=15_000_000, transcendentals=0
        ),
        name="gradient_first",
    )(hidden, in_all, solved, low_in, low_hid, *before)


def gradient_rest(hat_own, hat_other, in_all, solved_own, solved_other, low_in, token_count):
    tokens, columns = hat_own.shape
    parts, rows, _ = in_all.shape
    rank = low_in.shape[2]
    chunk, half = tokens // 2, columns // 2

    def first(i):
        return jnp.minimum(i, 1), 0

    def second(i):
        return jnp.maximum(i - 2, 0), 0

    return pl.pallas_call(
        functools.partial(rest_kernel, 1.0 / token_count),
        out_shape=[jax.ShapeDtypeStruct((3 * rows, half), bf16)] * 2,
        grid=(4,),
        in_specs=[
            pl.BlockSpec((chunk, columns), first),
            pl.BlockSpec((chunk, columns), second),
            pl.BlockSpec((parts, rows, chunk), lambda i: (0, 0, i)),
            pl.BlockSpec((chunk, 2 * rank), first),
            pl.BlockSpec((chunk, 2 * rank), second),
            pl.BlockSpec((parts, rows, rank), lambda i: (0, 0, 0)),
        ],
        out_specs=[pl.BlockSpec((3 * rows, half), lambda i: (0, 0))] * 2,
        scratch_shapes=[pltpu.VMEM((4 * rows, chunk), bf16)]
        + [pltpu.VMEM((3 * rows, half), f32)] * 2,
        compiler_params=pltpu.CompilerParams(vmem_limit_bytes=56 * 2**20),
        cost_estimate=pl.CostEstimate(
            flops=7_000_000_000, bytes_accessed=20_000_000, transcendentals=0
        ),
        name="gradient_rest",
    )(hat_own, hat_other, in_all, solved_own, solved_other, low_in)


def project_kernel(
    token_count, mine_ref, other_ref, omega_in_ref, omega_hid_ref, in_ref, hid_ref, both_ref, low_ref, blocks_ref, sketch_ref
):
    rank = sketch_ref.shape[0]
    me = lax.axis_index("c")
    sketch_ref[pl.ds(pl.multiple_of(me * (rank // 2), rank // 2), rank // 2), :] = mine_ref[...]
    sketch_ref[pl.ds(pl.multiple_of((1 - me) * (rank // 2), rank // 2), rank // 2), :] = other_ref[...]
    pieces = both_ref.shape[0]
    core_rows = 2 * rank // pieces
    tokens = in_ref.shape[0] // pieces
    start = 0
    for i, (omega, values) in enumerate(((omega_in_ref, in_ref), (omega_hid_ref, hid_ref))):
        end = start + values.shape[1]
        basis = sketch_ref[:, start:end]
        moment = jnp.dot(basis, omega[...], preferred_element_type=f32) / token_count
        square = row_product(basis, basis) / (float(token_count) * token_count)
        core = damping * 0.5 * (moment + moment.T) + square
        high = core.astype(bf16)
        rest = (core - high.astype(f32)).astype(bf16)
        low = (basis.astype(f32) / token_count).astype(bf16)
        if i == 0:
            turned = low.astype(f32).T.astype(bf16)
            block = blocks_ref.shape[1]
            for k in range(blocks_ref.shape[0]):
                blocks_ref[k] = turned[k * block : (k + 1) * block]
        else:
            low_ref[...] = low
        reach = row_product(values[...], low).astype(bf16)
        for k in range(pieces // 2):
            at = slice(k * core_rows, (k + 1) * core_rows)
            both_ref[i * pieces // 2 + k, :core_rows, :rank] = high[at]
            both_ref[i * pieces // 2 + k, :core_rows, rank:] = rest[at]
        for k in range(pieces):
            both_ref[k, core_rows:, i * rank : (i + 1) * rank] = reach[k * tokens : (k + 1) * tokens]
        start = end


def project(mine, other, omega_in, omega_hid, inputs, hidden_err, token_count):
    rank, width = 2 * mine.shape[0], mine.shape[1]
    tokens, local_in = inputs.shape
    rows = 2 * rank // N_MP + tokens // N_MP
    return pl.pallas_call(
        functools.partial(project_kernel, token_count),
        out_shape=[
            jax.ShapeDtypeStruct((N_MP, rows, 2 * rank), bf16),
            jax.ShapeDtypeStruct((rank, width - local_in), bf16),
            jax.ShapeDtypeStruct((4, local_in // 4, rank), bf16),
        ],
        in_specs=[pl.BlockSpec(memory_space=pltpu.VMEM)] * 6,
        out_specs=[pl.BlockSpec(memory_space=pltpu.VMEM)] * 3,
        scratch_shapes=[pltpu.VMEM((rank, width), bf16)],
        compiler_params=pltpu.CompilerParams(vmem_limit_bytes=24 * 2**20),
        name="project",
    )(mine, other, omega_in, omega_hid, inputs, hidden_err)


def two_halves(value):
    high = lax.reduce_precision(value, 8, 7)
    return jnp.concatenate([high.astype(bf16), (value - high).astype(bf16)], axis=-1)


def whole_value(halves):
    size = halves.shape[-1] // 2
    return halves[..., :size].astype(f32) + halves[..., size:].astype(f32)


def on_device(inputs, hidden_pre, hidden_grad, omega_in, omega_hid, owner_table):
    local_tokens, local_in = inputs.shape
    token_count = local_tokens * N_DP
    rank = omega_in.shape[1]
    block = local_in // 4
    near_tokens = 4 * local_tokens
    iy, ic, izh, izl = (lax.axis_index(a) for a in ("y", "c", "zh", "zl"))

    far = swap(inputs, "zl")

    hidden_err = (hidden_grad.astype(f32) * gelu_slope(hidden_pre)).astype(bf16)
    rows = jnp.concatenate(
        [
            jnp.dot(inputs, omega_in, preferred_element_type=f32).astype(bf16),
            jnp.dot(hidden_err, omega_hid, preferred_element_type=f32).astype(bf16),
        ],
        axis=1,
    )
    rows = after(rows.reshape(N_MP, local_tokens // N_MP, 2 * rank), far)
    rows = sum_scatter(rows, MP)
    near, far = (v.T.reshape(2, 2, block, local_tokens) for v in (inputs, far))
    for_y = []
    for k in range(4):
        to = (iy + k) % 4
        for_y.append(jnp.where(izl == to // 2, pick(near, to % 2), pick(far, to % 2)))
    in_parts = [for_y[0]] + [shift(for_y[k], "y", 4, k) for k in range(1, 4)]
    rows, in_parts[1], in_parts[3] = lax.optimization_barrier((rows, in_parts[1], in_parts[3]))
    rows = collect(rows, MP, N_MP).reshape(local_tokens, 2 * rank)
    rows, in_parts[2] = lax.optimization_barrier((rows, in_parts[2]))
    in_parts = jnp.stack(in_parts)
    in_parts = jnp.stack([pick(jnp.moveaxis(in_parts, 1, 0), ic), swap(pick(jnp.moveaxis(in_parts, 1, 0), 1 - ic), "c")])
    in_parts = [in_parts[:, k] for k in range(4)]

    sketch = jnp.concatenate(
        [
            token_product(rows[:, :rank], inputs).astype(bf16),
            token_product(rows[:, rank:], hidden_err).astype(bf16),
        ],
        axis=1,
    )
    in_near = line_up(in_parts, "y", 2)
    in_all = lax.all_gather(in_near, "x")

    width = sketch.shape[1]
    halves = sketch.reshape(2, rank // 2, width)
    part = pick(halves, ic).astype(f32) + swap(pick(halves, 1 - ic), "c").astype(f32)
    part = after(part.astype(bf16), in_near)
    part = sum_scatter(part.reshape(4, rank // 8, width), "y")
    part = sum_scatter(part.reshape(4, rank // 32, width), "zh")
    hid_own = lax.all_gather(hidden_err, "y").reshape(near_tokens, -1)
    part = collect(part, "zh", 4).reshape(rank // 8, width)
    part = collect(part, "y", 4).reshape(rank // 2, width)
    other = swap(part, "c")
    both, low_hid, low_blocks = project(
        part, other, omega_in, omega_hid, inputs, hidden_err, token_count
    )
    low_block = pick(low_blocks, (iy % 2) * 2 + ic)
    low_far = swap(low_block, "zl")
    both = exchange(after(both, in_all), MP)
    both, low_far = lax.optimization_barrier((both, low_far))
    low_block = jnp.where(izl == iy // 2, low_block, low_far)
    low_parts = [low_block] + [shift(low_block, "x", 4, k) for k in range(1, 4)]
    core_rows = 2 * rank // N_MP
    core = whole_value(both[:, :core_rows]).sum(0)
    reach = both[:, core_rows:].astype(f32).sum(0).astype(bf16)
    both = jnp.concatenate([two_halves(core), reach])
    both = collect(both, MP, N_MP)
    both, low_parts = lax.optimization_barrier((both, low_parts))
    reach = both[:, core_rows:].reshape(local_tokens, 2 * rank)

    reach_parts = [reach] + [shift(reach, "y", 4, k) for k in range(1, 4)]
    owner = owner_table[lax.axis_index(DP)]
    held, inverse = factor_and_inverse(owner, both, rank)
    inverse, reach_parts, hid_own = lax.optimization_barrier((inverse, reach_parts, hid_own))
    hid_other = swap(hid_own, "c")
    solved_own, low_in = solve(reach_parts, low_parts, inverse)
    solved_own = solved_own.reshape(near_tokens, 2 * rank)
    solved_other = swap(solved_own, "c")
    hat_own, up, down = gradient_first(
        0, hid_own, in_all, solved_own, low_in, low_hid, (), token_count
    )
    up, down, hid_other, solved_other = lax.optimization_barrier(
        (up, down, hid_other, solved_other)
    )
    hat_other, up, down = gradient_first(
        1, hid_other, in_all, solved_other, low_in, low_hid, (up, down), token_count
    )
    more_up, more_down = gradient_rest(
        hat_own, hat_other, in_all, solved_own, solved_other, low_in, token_count
    )
    quarter = up.shape[1] // 2
    done = []
    for value, more, turn, order in ((up, more_up, 1, (2, 0, 1)), (down, more_down, 3, (1, 2, 0))):
        for k in range(2):
            columns = slice(k * quarter, (k + 1) * quarter)
            running = value[:, columns]
            for at in order:
                running = shift(running, "zh", 4, turn).astype(f32)
                here = more[at * block : (at + 1) * block, columns].astype(f32)
                running = (running + here).astype(bf16)
            done.append(running)
    return (jnp.concatenate(done, axis=1), held)


def solution(mesh):
    parts = Mesh(
        mesh.devices.reshape([size for _, size in PARTS]), [name for name, _ in PARTS]
    )
    return jax.shard_map(
        on_device,
        mesh=parts,
        in_specs=(P(DP, MP), P(DP, MP), P(DP, MP), P(MP, None), P(MP, None), P()),
        out_specs=(P(DP, MP), P(DP, None, None)),
        check_vma=False,
    )
```

```python
import functools

import jax
import jax.numpy as jnp
from jax import lax
from jax.experimental import pallas as pl
from jax.experimental.pallas import tpu as pltpu
from jax.sharding import Mesh
from jax.sharding import PartitionSpec as P

damping = 0.25
half_root = 0.7071067811865476
inverse_root_tau = 0.3989422804014327

PARTS = (("zh", 4), ("y", 4), ("c", 2), ("x", 4), ("zl", 2))
DP = ("zh", "y", "c")
MP = ("x", "zl")
N_DP = 32
N_MP = 8
PANEL = 64
GROUP = 16
bf16 = jnp.bfloat16
f32 = jnp.float32


def gelu_slope(pre_values):
    values = pre_values.astype(f32)
    return (
        0.5 * (1.0 + lax.erf(values * half_root))
        + values * jnp.exp(-0.5 * values * values) * inverse_root_tau
    )


def token_product(left_side, right_side):
    return lax.dot_general(
        left_side, right_side, (((0,), (0,)), ((), ())), preferred_element_type=f32
    )


def row_product(left_side, right_side):
    return lax.dot_general(
        left_side, right_side, (((1,), (1,)), ((), ())), preferred_element_type=f32
    )


def exact_dot(left_side, right_side, dims):
    return lax.dot_general(
        left_side,
        right_side,
        (dims, ((), ())),
        precision=lax.Precision.HIGHEST,
        preferred_element_type=f32,
    )


def exchange(parts, axis):
    return lax.all_to_all(parts, axis, 0, 0)


def sum_scatter(parts, axis):
    return exchange(parts, axis).astype(f32).sum(0).astype(bf16)


def collect(part, axis, count):
    return exchange(jnp.broadcast_to(part[None], (count,) + part.shape), axis)


def shift(value, axis, count, step):
    return lax.ppermute(value, axis, [(i, (i + step) % count) for i in range(count)])


def swap(value, axis):
    return lax.ppermute(value, axis, [(0, 1), (1, 0)])


def pick(stack, index):
    return lax.dynamic_index_in_dim(stack, index, 0, False)


def after(value, *others):
    return lax.optimization_barrier((value,) + others)[0]


def line_up(parts, axis, pieces):
    count = len(parts)
    rows, columns = parts[0].shape[1:]
    if pieces == 1:
        shape = (count, rows, columns)
    else:
        shape = (rows, pieces * count * columns)

    def kernel(*refs):
        part_refs, out_ref, sems = refs[:count], refs[count], refs[count + 1]
        me = lax.axis_index(axis)
        copies = []
        for k in range(count):
            at = lax.rem(me - k + count, count)
            for piece in range(pieces):
                if pieces == 1:
                    target = out_ref.at[at]
                else:
                    start = pl.multiple_of((piece * count + at) * columns, columns)
                    target = out_ref.at[:, pl.ds(start, columns)]
                copies.append(
                    pltpu.make_async_copy(
                        part_refs[k].at[piece], target, sems.at[k * pieces + piece]
                    )
                )
        for copy in copies:
            copy.start()
        for copy in copies:
            copy.wait()

    return pl.pallas_call(
        kernel,
        out_shape=jax.ShapeDtypeStruct(shape, parts[0].dtype),
        in_specs=[pl.BlockSpec(memory_space=pl.ANY)] * count,
        out_specs=pl.BlockSpec(memory_space=pltpu.HBM),
        scratch_shapes=[pltpu.SemaphoreType.DMA((count * pieces,))],
        compiler_params=pltpu.CompilerParams(vmem_limit_bytes=2**20),
        name="line_up",
    )(*parts)


def eliminate(block):
    size = block.shape[0]
    rows = lax.broadcasted_iota(jnp.int32, (size, size), 0)
    lanes = lax.broadcasted_iota(jnp.int32, (size, size), 1)
    work = jnp.concatenate([block, (lanes == rows).astype(f32)], axis=1)
    row_ids = lax.broadcasted_iota(jnp.int32, (size, 2 * size), 0)
    inverse_pivots = []
    for first in range(0, size, GROUP):
        columns = [
            jnp.broadcast_to(work[:, first + k : first + k + 1], (size, 2 * size))
            for k in range(GROUP)
        ]
        heads = [work[first + k : first + k + 1, :] for k in range(GROUP)]
        for k in range(GROUP):
            at = first + k
            inverse = 1.0 / columns[k][at : at + 1, :]
            inverse_pivots.append(inverse)
            factor = jnp.where(row_ids > at, columns[k] * inverse, 0.0)
            work = work - factor * heads[k]
            for later in range(k + 1, GROUP):
                columns[later] = columns[later] - factor * columns[later][at : at + 1, :]
                heads[later] = (
                    heads[later] - factor[first + later : first + later + 1, :] * heads[k]
                )
    return (work * jnp.sqrt(jnp.concatenate(inverse_pivots, axis=0)))[:, size:]


def factor_kernel(owner_ref, both_ref, held_ref, inverse_ref, work):
    count, size, _ = inverse_ref.shape
    pieces = both_ref.shape[0] // count
    piece = size // pieces
    rows = lax.broadcasted_iota(jnp.int32, (size, size), 0)
    lanes = lax.broadcasted_iota(jnp.int32, (size, size), 1)
    for i in range(count):
        for k in range(pieces):
            halves = both_ref[i * pieces + k, :piece, :].astype(f32)
            work[i, k * piece : (k + 1) * piece, :size] = halves[:, :size] + halves[:, size:]
        work[i, :, size:] = (rows == lanes).astype(f32)
    for low in range(0, size, PANEL):
        high = low + PANEL
        panels = []
        for i in range(count):
            small = eliminate(work[i, low:high, low:high])
            panel = exact_dot(small, work[i, low:high, :], ((1,), (0,)))
            work[i, low:high, :] = panel
            panels.append(panel)
        if high < size:
            for i in range(count):
                work[i, high:, :] = work[i, high:, :] - exact_dot(
                    panels[i][:, high:size], panels[i], ((0,), (0,))
                )
    for i in range(count):
        @pl.when(owner_ref[0] == i)
        def _(i=i):
            held_ref[0] = jnp.where(rows <= lanes, work[i, :, :size], 0.0).T

        inverse_ref[i] = exact_dot(work[i, :, size:], work[i, :, size:], ((0,), (0,)))


def factor_and_inverse(owner, both, size):
    return pl.pallas_call(
        factor_kernel,
        out_shape=[
            jax.ShapeDtypeStruct((1, size, size), f32),
            jax.ShapeDtypeStruct((2, size, size), f32),
        ],
        in_specs=[
            pl.BlockSpec(memory_space=pltpu.SMEM),
            pl.BlockSpec(memory_space=pltpu.VMEM),
        ],
        out_specs=[pl.BlockSpec(memory_space=pltpu.VMEM)] * 2,
        scratch_shapes=[pltpu.VMEM((2, size, 2 * size), f32)],
        compiler_params=pltpu.CompilerParams(vmem_limit_bytes=16 * 2**20),
        cost_estimate=pl.CostEstimate(
            flops=12 * size**3, bytes_accessed=60_000_000, transcendentals=0
        ),
        name="factor_and_inverse",
    )(owner, both)


def solve_kernel(*refs):
    reach_refs, low_refs, inverse_ref, out_ref, low_ref = refs[:4], refs[4:8], *refs[8:]
    size = inverse_ref.shape[1]
    iy, ix = lax.axis_index("y"), lax.axis_index("x")
    inverses = []
    for i in range(2):
        rest, pieces = inverse_ref[i], []
        for _ in range(3):
            pieces.append(rest.astype(bf16))
            rest = rest - pieces[-1].astype(f32)
        inverses.append(pieces)
    for k in range(4):
        low_ref[lax.rem(ix - k + 4, 4)] = low_refs[k][...]
        at = lax.rem(iy - k + 4, 4)
        for i in range(2):
            reach = reach_refs[k][:, i * size : (i + 1) * size]
            solved = sum(
                jnp.dot(reach, piece, preferred_element_type=f32) for piece in inverses[i][::-1]
            )
            out_ref[at, :, i * size : (i + 1) * size] = solved.astype(bf16)


def solve(reach_parts, low_parts, inverse):
    return pl.pallas_call(
        solve_kernel,
        out_shape=[
            jax.ShapeDtypeStruct((4,) + reach_parts[0].shape, bf16),
            jax.ShapeDtypeStruct((4,) + low_parts[0].shape, bf16),
        ],
        in_specs=[pl.BlockSpec(memory_space=pltpu.VMEM)] * 9,
        out_specs=[pl.BlockSpec(memory_space=pltpu.VMEM)] * 2,
        compiler_params=pltpu.CompilerParams(vmem_limit_bytes=16 * 2**20),
        name="solve",
    )(*reach_parts, *low_parts, inverse)


def removed(values, taken):
    return ((values.astype(f32) - taken) * (1.0 / damping)).astype(bf16)


def add_term(total, term, step):
    @pl.when(step == 0)
    def _():
        total[...] = term

    @pl.when(step > 0)
    def _():
        total[...] = total[...] + term


def first_kernel(scale, hidden_ref, in_ref, solved_ref, low_in_ref, low_hid_ref, *refs):
    before, (hat_ref, up_ref, down_ref, up_total, down_total) = refs[:-5], refs[-5:]
    step, steps = pl.program_id(0), pl.num_programs(0)
    me = lax.axis_index("zh")
    rank, columns = low_hid_ref.shape
    taken = jnp.dot(solved_ref[:, rank:], low_hid_ref[...], preferred_element_type=f32)
    hat_hid = removed(hidden_ref[...], taken)
    hat_ref[...] = hat_hid
    for total, off, start in ((up_total, 3, 0), (down_total, 1, columns // 2)):
        at = lax.rem(me + off, 4)
        hat_in = removed(in_ref[at], row_product(low_in_ref[at], solved_ref[:, :rank]))
        part = hat_hid[:, start : start + columns // 2]
        add_term(total, jnp.dot(hat_in, part, preferred_element_type=f32), step)

    @pl.when(step == steps - 1)
    def _():
        up, down = up_total[...], down_total[...]
        if before:
            up, down = up + before[0][...], down + before[1][...]
        up_ref[...] = (up * scale).astype(up_ref.dtype)
        down_ref[...] = (down * scale).astype(down_ref.dtype)


def rest_kernel(
    scale, hat_own_ref, hat_other_ref, in_ref, solved_own_ref, solved_other_ref, low_in_ref, up_ref, down_ref, hat_in, up_total, down_total
):
    step, steps = pl.program_id(0), pl.num_programs(0)
    me = lax.axis_index("zh")
    rank, columns = low_in_ref.shape[2], hat_own_ref.shape[1]
    rows = in_ref.shape[1]

    def body(hat_ref, solved_ref):
        for k, off in enumerate((1, 0, 2, 3)):
            at = lax.rem(me + off, 4)
            taken = row_product(low_in_ref[at], solved_ref[:, :rank])
            hat_in[k * rows : (k + 1) * rows, :] = removed(in_ref[at], taken)
        for total, low, start in ((up_total, 0, 0), (down_total, rows, columns // 2)):
            term = jnp.dot(
                hat_in[low : low + 3 * rows, :],
                hat_ref[:, start : start + columns // 2],
                preferred_element_type=f32,
            )
            add_term(total, term, step)

    pl.when(step < steps // 2)(functools.partial(body, hat_own_ref, solved_own_ref))
    pl.when(step >= steps // 2)(functools.partial(body, hat_other_ref, solved_other_ref))

    @pl.when(step == steps - 1)
    def _():
        up_ref[...] = (up_total[...] * scale).astype(bf16)
        down_ref[...] = (down_total[...] * scale).astype(bf16)


def gradient_first(core, hidden, in_all, solved, low_in, low_hid, before, token_count):
    tokens, columns = hidden.shape
    parts, rows, _ = in_all.shape
    rank = low_hid.shape[0]
    chunk, half = tokens // 2, columns // 2
    last = len(before) > 0
    block_spec = pl.BlockSpec((rows, half), lambda i: (0, 0))
    return pl.pallas_call(
        functools.partial(first_kernel, 1.0 / token_count if last else 1.0),
        out_shape=[
            jax.ShapeDtypeStruct((tokens, columns), bf16),
            jax.ShapeDtypeStruct((rows, half), bf16 if last else f32),
            jax.ShapeDtypeStruct((rows, half), bf16 if last else f32),
        ],
        grid=(2,),
        in_specs=[
            pl.BlockSpec((chunk, columns), lambda i: (i, 0)),
            pl.BlockSpec((parts, rows, chunk), lambda i: (0, 0, 2 * core + i)),
            pl.BlockSpec((chunk, 2 * rank), lambda i: (i, 0)),
            pl.BlockSpec((parts, rows, rank), lambda i: (0, 0, 0)),
            pl.BlockSpec((rank, columns), lambda i: (0, 0)),
        ]
        + [block_spec] * len(before),
        out_specs=[pl.BlockSpec((chunk, columns), lambda i: (i, 0)), block_spec, block_spec],
        scratch_shapes=[pltpu.VMEM((rows, half), f32)] * 2,
        compiler_params=pltpu.CompilerParams(vmem_limit_bytes=48 * 2**20),
        cost_estimate=pl.CostEstimate(
            flops=2_500_000_000, bytes_accessed=15_000_000, transcendentals=0
        ),
        name="gradient_first",
    )(hidden, in_all, solved, low_in, low_hid, *before)


def gradient_rest(hat_own, hat_other, in_all, solved_own, solved_other, low_in, token_count):
    tokens, columns = hat_own.shape
    parts, rows, _ = in_all.shape
    rank = low_in.shape[2]
    chunk, half = tokens // 2, columns // 2

    def first(i):
        return jnp.minimum(i, 1), 0

    def second(i):
        return jnp.maximum(i - 2, 0), 0

    return pl.pallas_call(
        functools.partial(rest_kernel, 1.0 / token_count),
        out_shape=[jax.ShapeDtypeStruct((3 * rows, half), bf16)] * 2,
        grid=(4,),
        in_specs=[
            pl.BlockSpec((chunk, columns), first),
            pl.BlockSpec((chunk, columns), second),
            pl.BlockSpec((parts, rows, chunk), lambda i: (0, 0, i)),
            pl.BlockSpec((chunk, 2 * rank), first),
            pl.BlockSpec((chunk, 2 * rank), second),
            pl.BlockSpec((parts, rows, rank), lambda i: (0, 0, 0)),
        ],
        out_specs=[pl.BlockSpec((3 * rows, half), lambda i: (0, 0))] * 2,
        scratch_shapes=[pltpu.VMEM((4 * rows, chunk), bf16)]
        + [pltpu.VMEM((3 * rows, half), f32)] * 2,
        compiler_params=pltpu.CompilerParams(vmem_limit_bytes=48 * 2**20),
        cost_estimate=pl.CostEstimate(
            flops=7_000_000_000, bytes_accessed=20_000_000, transcendentals=0
        ),
        name="gradient_rest",
    )(hat_own, hat_other, in_all, solved_own, solved_other, low_in)


def project_kernel(
    token_count, mine_ref, other_ref, omega_in_ref, omega_hid_ref, in_ref, hid_ref, both_ref, low_ref, blocks_ref, sketch_ref
):
    rank = sketch_ref.shape[0]
    me = lax.axis_index("c")
    sketch_ref[pl.ds(pl.multiple_of(me * (rank // 2), rank // 2), rank // 2), :] = mine_ref[...]
    sketch_ref[pl.ds(pl.multiple_of((1 - me) * (rank // 2), rank // 2), rank // 2), :] = other_ref[...]
    pieces = both_ref.shape[0]
    core_rows = 2 * rank // pieces
    tokens = in_ref.shape[0] // pieces
    start = 0
    for i, (omega, values) in enumerate(((omega_in_ref, in_ref), (omega_hid_ref, hid_ref))):
        end = start + values.shape[1]
        basis = sketch_ref[:, start:end]
        moment = jnp.dot(basis, omega[...], preferred_element_type=f32) / token_count
        square = row_product(basis, basis) / (float(token_count) * token_count)
        core = damping * 0.5 * (moment + moment.T) + square
        high = core.astype(bf16)
        rest = (core - high.astype(f32)).astype(bf16)
        low = (basis.astype(f32) / token_count).astype(bf16)
        if i == 0:
            turned = low.astype(f32).T.astype(bf16)
            block = blocks_ref.shape[1]
            for k in range(blocks_ref.shape[0]):
                blocks_ref[k] = turned[k * block : (k + 1) * block]
        else:
            low_ref[...] = low
        reach = row_product(values[...], low).astype(bf16)
        for k in range(pieces // 2):
            at = slice(k * core_rows, (k + 1) * core_rows)
            both_ref[i * pieces // 2 + k, :core_rows, :rank] = high[at]
            both_ref[i * pieces // 2 + k, :core_rows, rank:] = rest[at]
        for k in range(pieces):
            both_ref[k, core_rows:, i * rank : (i + 1) * rank] = reach[k * tokens : (k + 1) * tokens]
        start = end


def project(mine, other, omega_in, omega_hid, inputs, hidden_err, token_count):
    rank, width = 2 * mine.shape[0], mine.shape[1]
    tokens, local_in = inputs.shape
    rows = 2 * rank // N_MP + tokens // N_MP
    return pl.pallas_call(
        functools.partial(project_kernel, token_count),
        out_shape=[
            jax.ShapeDtypeStruct((N_MP, rows, 2 * rank), bf16),
            jax.ShapeDtypeStruct((rank, width - local_in), bf16),
            jax.ShapeDtypeStruct((4, local_in // 4, rank), bf16),
        ],
        in_specs=[pl.BlockSpec(memory_space=pltpu.VMEM)] * 6,
        out_specs=[pl.BlockSpec(memory_space=pltpu.VMEM)] * 3,
        scratch_shapes=[pltpu.VMEM((rank, width), bf16)],
        compiler_params=pltpu.CompilerParams(vmem_limit_bytes=24 * 2**20),
        name="project",
    )(mine, other, omega_in, omega_hid, inputs, hidden_err)


def two_halves(value):
    high = lax.reduce_precision(value, 8, 7)
    return jnp.concatenate([high.astype(bf16), (value - high).astype(bf16)], axis=-1)


def whole_value(halves):
    size = halves.shape[-1] // 2
    return halves[..., :size].astype(f32) + halves[..., size:].astype(f32)


def on_device(inputs, hidden_pre, hidden_grad, omega_in, omega_hid, owner_table):
    local_tokens, local_in = inputs.shape
    token_count = local_tokens * N_DP
    rank = omega_in.shape[1]
    block = local_in // 4
    near_tokens = 4 * local_tokens
    iy, ic, izh, izl = (lax.axis_index(a) for a in ("y", "c", "zh", "zl"))

    far = swap(inputs, "zl")

    hidden_err = (hidden_grad.astype(f32) * gelu_slope(hidden_pre)).astype(bf16)
    rows = jnp.concatenate(
        [
            jnp.dot(inputs, omega_in, preferred_element_type=f32).astype(bf16),
            jnp.dot(hidden_err, omega_hid, preferred_element_type=f32).astype(bf16),
        ],
        axis=1,
    )
    rows = after(rows.reshape(N_MP, local_tokens // N_MP, 2 * rank), far)
    rows = sum_scatter(rows, MP)
    near, far = (v.T.reshape(2, 2, block, local_tokens) for v in (inputs, far))
    for_y = []
    for k in range(4):
        to = (iy + k) % 4
        for_y.append(jnp.where(izl == to // 2, pick(near, to % 2), pick(far, to % 2)))
    in_parts = [for_y[0]] + [shift(for_y[k], "y", 4, k) for k in range(1, 4)]
    rows, in_parts[1], in_parts[3] = lax.optimization_barrier((rows, in_parts[1], in_parts[3]))
    rows = collect(rows, MP, N_MP).reshape(local_tokens, 2 * rank)
    rows, in_parts[2] = lax.optimization_barrier((rows, in_parts[2]))
    in_parts = jnp.stack(in_parts)
    in_parts = jnp.stack([pick(jnp.moveaxis(in_parts, 1, 0), ic), swap(pick(jnp.moveaxis(in_parts, 1, 0), 1 - ic), "c")])
    in_parts = [in_parts[:, k] for k in range(4)]

    sketch = jnp.concatenate(
        [
            token_product(rows[:, :rank], inputs).astype(bf16),
            token_product(rows[:, rank:], hidden_err).astype(bf16),
        ],
        axis=1,
    )
    in_near = line_up(in_parts, "y", 2)
    in_all = lax.all_gather(in_near, "x")

    width = sketch.shape[1]
    halves = sketch.reshape(2, rank // 2, width)
    part = pick(halves, ic).astype(f32) + swap(pick(halves, 1 - ic), "c").astype(f32)
    part = after(part.astype(bf16), in_near)
    part = sum_scatter(part.reshape(4, rank // 8, width), "y")
    part = sum_scatter(part.reshape(4, rank // 32, width), "zh")
    hid_own = lax.all_gather(hidden_err, "y").reshape(near_tokens, -1)
    part = collect(part, "zh", 4).reshape(rank // 8, width)
    part = collect(part, "y", 4).reshape(rank // 2, width)
    other = swap(part, "c")
    both, low_hid, low_blocks = project(
        part, other, omega_in, omega_hid, inputs, hidden_err, token_count
    )
    low_block = pick(low_blocks, (iy % 2) * 2 + ic)
    low_far = swap(low_block, "zl")
    both = exchange(after(both, in_all), MP)
    both, low_far = lax.optimization_barrier((both, low_far))
    low_block = jnp.where(izl == iy // 2, low_block, low_far)
    low_parts = [low_block] + [shift(low_block, "x", 4, k) for k in range(1, 4)]
    core_rows = 2 * rank // N_MP
    core = whole_value(both[:, :core_rows]).sum(0)
    reach = both[:, core_rows:].astype(f32).sum(0).astype(bf16)
    both = jnp.concatenate([two_halves(core), reach])
    both = collect(both, MP, N_MP)
    both, low_parts = lax.optimization_barrier((both, low_parts))
    reach = both[:, core_rows:].reshape(local_tokens, 2 * rank)

    reach_parts = [reach] + [shift(reach, "y", 4, k) for k in range(1, 4)]
    owner = owner_table[lax.axis_index(DP)]
    held, inverse = factor_and_inverse(owner, both, rank)
    inverse, reach_parts, hid_own = lax.optimization_barrier((inverse, reach_parts, hid_own))
    hid_other = swap(hid_own, "c")
    solved_own, low_in = solve(reach_parts, low_parts, inverse)
    solved_own = solved_own.reshape(near_tokens, 2 * rank)
    solved_other = swap(solved_own, "c")
    hat_own, up, down = gradient_first(
        0, hid_own, in_all, solved_own, low_in, low_hid, (), token_count
    )
    up, down, hid_other, solved_other = lax.optimization_barrier(
        (up, down, hid_other, solved_other)
    )
    hat_other, up, down = gradient_first(
        1, hid_other, in_all, solved_other, low_in, low_hid, (up, down), token_count
    )
    more_up, more_down = gradient_rest(
        hat_own, hat_other, in_all, solved_own, solved_other, low_in, token_count
    )
    quarter = up.shape[1] // 2
    done = []
    for value, more, turn, order in ((up, more_up, 1, (2, 0, 1)), (down, more_down, 3, (1, 2, 0))):
        for k in range(2):
            columns = slice(k * quarter, (k + 1) * quarter)
            running = value[:, columns]
            for at in order:
                running = shift(running, "zh", 4, turn).astype(f32)
                here = more[at * block : (at + 1) * block, columns].astype(f32)
                running = (running + here).astype(bf16)
            done.append(running)
    return (jnp.concatenate(done, axis=1), held)


def solution(mesh):
    parts = Mesh(
        mesh.devices.reshape([size for _, size in PARTS]), [name for name, _ in PARTS]
    )
    return jax.shard_map(
        on_device,
        mesh=parts,
        in_specs=(P(DP, MP), P(DP, MP), P(DP, MP), P(MP, None), P(MP, None), P()),
        out_specs=(P(DP, MP), P(DP, None, None)),
        check_vma=False,
    )
```

```python
import functools

import jax
import jax.numpy as jnp
from jax import lax
from jax.experimental import pallas as pl
from jax.experimental.pallas import tpu as pltpu
from jax.sharding import Mesh
from jax.sharding import PartitionSpec as P

damping = 0.25
half_root = 0.7071067811865476
inverse_root_tau = 0.3989422804014327

PARTS = (("zh", 4), ("y", 4), ("c", 2), ("x", 4), ("zl", 2))
DP = ("zh", "y", "c")
MP = ("x", "zl")
N_DP = 32
N_MP = 8
PANEL = 64
GROUP = 16
bf16 = jnp.bfloat16
f32 = jnp.float32


def gelu_slope(pre_values):
    values = pre_values.astype(f32)
    return (
        0.5 * (1.0 + lax.erf(values * half_root))
        + values * jnp.exp(-0.5 * values * values) * inverse_root_tau
    )


def token_product(left_side, right_side):
    return lax.dot_general(
        left_side, right_side, (((0,), (0,)), ((), ())), preferred_element_type=f32
    )


def row_product(left_side, right_side):
    return lax.dot_general(
        left_side, right_side, (((1,), (1,)), ((), ())), preferred_element_type=f32
    )


def exact_dot(left_side, right_side, dims):
    return lax.dot_general(
        left_side,
        right_side,
        (dims, ((), ())),
        precision=lax.Precision.HIGHEST,
        preferred_element_type=f32,
    )


def exchange(parts, axis):
    return lax.all_to_all(parts, axis, 0, 0)


def sum_scatter(parts, axis):
    return exchange(parts, axis).astype(f32).sum(0).astype(bf16)


def collect(part, axis, count):
    return exchange(jnp.broadcast_to(part[None], (count,) + part.shape), axis)


def shift(value, axis, count, step):
    return lax.ppermute(value, axis, [(i, (i + step) % count) for i in range(count)])


def swap(value, axis):
    return lax.ppermute(value, axis, [(0, 1), (1, 0)])


def pick(stack, index):
    return lax.dynamic_index_in_dim(stack, index, 0, False)


def after(value, *others):
    return lax.optimization_barrier((value,) + others)[0]


def line_up(parts, axis, pieces):
    count = len(parts)
    rows, columns = parts[0].shape[1:]
    if pieces == 1:
        shape = (count, rows, columns)
    else:
        shape = (rows, pieces * count * columns)

    def kernel(*refs):
        part_refs, out_ref, sems = refs[:count], refs[count], refs[count + 1]
        me = lax.axis_index(axis)
        copies = []
        for k in range(count):
            at = lax.rem(me - k + count, count)
            for piece in range(pieces):
                if pieces == 1:
                    target = out_ref.at[at]
                else:
                    start = pl.multiple_of((piece * count + at) * columns, columns)
                    target = out_ref.at[:, pl.ds(start, columns)]
                copies.append(
                    pltpu.make_async_copy(
                        part_refs[k].at[piece], target, sems.at[k * pieces + piece]
                    )
                )
        for copy in copies:
            copy.start()
        for copy in copies:
            copy.wait()

    return pl.pallas_call(
        kernel,
        out_shape=jax.ShapeDtypeStruct(shape, parts[0].dtype),
        in_specs=[pl.BlockSpec(memory_space=pl.ANY)] * count,
        out_specs=pl.BlockSpec(memory_space=pltpu.HBM),
        scratch_shapes=[pltpu.SemaphoreType.DMA((count * pieces,))],
        compiler_params=pltpu.CompilerParams(vmem_limit_bytes=2**20),
        name="line_up",
    )(*parts)


def eliminate(block):
    size = block.shape[0]
    rows = lax.broadcasted_iota(jnp.int32, (size, size), 0)
    lanes = lax.broadcasted_iota(jnp.int32, (size, size), 1)
    work = jnp.concatenate([block, (lanes == rows).astype(f32)], axis=1)
    row_ids = lax.broadcasted_iota(jnp.int32, (size, 2 * size), 0)
    inverse_pivots = []
    for first in range(0, size, GROUP):
        columns = [
            jnp.broadcast_to(work[:, first + k : first + k + 1], (size, 2 * size))
            for k in range(GROUP)
        ]
        heads = [work[first + k : first + k + 1, :] for k in range(GROUP)]
        for k in range(GROUP):
            at = first + k
            inverse = 1.0 / columns[k][at : at + 1, :]
            inverse_pivots.append(inverse)
            factor = jnp.where(row_ids > at, columns[k] * inverse, 0.0)
            work = work - factor * heads[k]
            for later in range(k + 1, GROUP):
                columns[later] = columns[later] - factor * columns[later][at : at + 1, :]
                heads[later] = (
                    heads[later] - factor[first + later : first + later + 1, :] * heads[k]
                )
    return (work * jnp.sqrt(jnp.concatenate(inverse_pivots, axis=0)))[:, size:]


def factor_kernel(owner_ref, both_ref, held_ref, inverse_ref, work):
    count, size, _ = inverse_ref.shape
    pieces = both_ref.shape[0] // count
    piece = size // pieces
    rows = lax.broadcasted_iota(jnp.int32, (size, size), 0)
    lanes = lax.broadcasted_iota(jnp.int32, (size, size), 1)
    for i in range(count):
        for k in range(pieces):
            halves = both_ref[i * pieces + k, :piece, :].astype(f32)
            work[i, k * piece : (k + 1) * piece, :size] = halves[:, :size] + halves[:, size:]
        work[i, :, size:] = (rows == lanes).astype(f32)
    for low in range(0, size, PANEL):
        high = low + PANEL
        panels = []
        for i in range(count):
            small = eliminate(work[i, low:high, low:high])
            panel = exact_dot(small, work[i, low:high, :], ((1,), (0,)))
            work[i, low:high, :] = panel
            panels.append(panel)
        if high < size:
            for i in range(count):
                work[i, high:, :] = work[i, high:, :] - exact_dot(
                    panels[i][:, high:size], panels[i], ((0,), (0,))
                )
    for i in range(count):
        @pl.when(owner_ref[0] == i)
        def _(i=i):
            held_ref[0] = jnp.where(rows <= lanes, work[i, :, :size], 0.0).T

        inverse_ref[i] = exact_dot(work[i, :, size:], work[i, :, size:], ((0,), (0,)))


def factor_and_inverse(owner, both, size):
    return pl.pallas_call(
        factor_kernel,
        out_shape=[
            jax.ShapeDtypeStruct((1, size, size), f32),
            jax.ShapeDtypeStruct((2, size, size), f32),
        ],
        in_specs=[
            pl.BlockSpec(memory_space=pltpu.SMEM),
            pl.BlockSpec(memory_space=pltpu.VMEM),
        ],
        out_specs=[pl.BlockSpec(memory_space=pltpu.VMEM)] * 2,
        scratch_shapes=[pltpu.VMEM((2, size, 2 * size), f32)],
        compiler_params=pltpu.CompilerParams(vmem_limit_bytes=16 * 2**20),
        cost_estimate=pl.CostEstimate(
            flops=12 * size**3, bytes_accessed=60_000_000, transcendentals=0
        ),
        name="factor_and_inverse",
    )(owner, both)


def solve_kernel(*refs):
    reach_refs, low_refs, inverse_ref, out_ref, low_ref = refs[:4], refs[4:8], *refs[8:]
    size = inverse_ref.shape[1]
    iy, ix = lax.axis_index("y"), lax.axis_index("x")
    inverses = []
    for i in range(2):
        rest, pieces = inverse_ref[i], []
        for _ in range(3):
            pieces.append(rest.astype(bf16))
            rest = rest - pieces[-1].astype(f32)
        inverses.append(pieces)
    for k in range(4):
        low_ref[lax.rem(ix - k + 4, 4)] = low_refs[k][...]
        at = lax.rem(iy - k + 4, 4)
        for i in range(2):
            reach = reach_refs[k][:, i * size : (i + 1) * size]
            solved = sum(
                jnp.dot(reach, piece, preferred_element_type=f32) for piece in inverses[i][::-1]
            )
            out_ref[at, :, i * size : (i + 1) * size] = solved.astype(bf16)


def solve(reach_parts, low_parts, inverse):
    return pl.pallas_call(
        solve_kernel,
        out_shape=[
            jax.ShapeDtypeStruct((4,) + reach_parts[0].shape, bf16),
            jax.ShapeDtypeStruct((4,) + low_parts[0].shape, bf16),
        ],
        in_specs=[pl.BlockSpec(memory_space=pltpu.VMEM)] * 9,
        out_specs=[pl.BlockSpec(memory_space=pltpu.VMEM)] * 2,
        compiler_params=pltpu.CompilerParams(vmem_limit_bytes=16 * 2**20),
        name="solve",
    )(*reach_parts, *low_parts, inverse)


def removed(values, taken):
    return ((values.astype(f32) - taken) * (1.0 / damping)).astype(bf16)


def add_term(total, term, step):
    @pl.when(step == 0)
    def _():
        total[...] = term

    @pl.when(step > 0)
    def _():
        total[...] = total[...] + term


def first_kernel(scale, hidden_ref, in_ref, solved_ref, low_in_ref, low_hid_ref, *refs):
    before, (hat_ref, up_ref, down_ref, up_total, down_total) = refs[:-5], refs[-5:]
    step, steps = pl.program_id(0), pl.num_programs(0)
    me = lax.axis_index("zh")
    rank, columns = low_hid_ref.shape
    taken = jnp.dot(solved_ref[:, rank:], low_hid_ref[...], preferred_element_type=f32)
    hat_hid = removed(hidden_ref[...], taken)
    hat_ref[...] = hat_hid
    for total, off, start in ((up_total, 3, 0), (down_total, 1, columns // 2)):
        at = lax.rem(me + off, 4)
        hat_in = removed(in_ref[at], row_product(low_in_ref[at], solved_ref[:, :rank]))
        part = hat_hid[:, start : start + columns // 2]
        add_term(total, jnp.dot(hat_in, part, preferred_element_type=f32), step)

    @pl.when(step == steps - 1)
    def _():
        up, down = up_total[...], down_total[...]
        if before:
            up, down = up + before[0][...], down + before[1][...]
        up_ref[...] = (up * scale).astype(up_ref.dtype)
        down_ref[...] = (down * scale).astype(down_ref.dtype)


def rest_kernel(
    scale, offsets, hat_own_ref, hat_other_ref, in_ref, solved_own_ref, solved_other_ref, low_in_ref, up_ref, down_ref, hat_in, up_total, down_total
):
    step, steps = pl.program_id(0), pl.num_programs(0)
    me = lax.axis_index("zh")
    rank, columns = low_in_ref.shape[2], hat_own_ref.shape[1]
    rows = in_ref.shape[1]

    def body(hat_ref, solved_ref):
        for k, off in enumerate(offsets):
            at = lax.rem(me + off, 4)
            taken = row_product(low_in_ref[at], solved_ref[:, :rank])
            hat_in[k * rows : (k + 1) * rows, :] = removed(in_ref[at], taken)
        size = up_total.shape[0]
        last = hat_in.shape[0] - size
        for total, low, start in ((up_total, 0, 0), (down_total, last, columns // 2)):
            term = jnp.dot(
                hat_in[low : low + size, :],
                hat_ref[:, start : start + columns // 2],
                preferred_element_type=f32,
            )
            add_term(total, term, step)

    pl.when(step < steps // 2)(functools.partial(body, hat_own_ref, solved_own_ref))
    pl.when(step >= steps // 2)(functools.partial(body, hat_other_ref, solved_other_ref))

    @pl.when(step == steps - 1)
    def _():
        up_ref[...] = (up_total[...] * scale).astype(bf16)
        down_ref[...] = (down_total[...] * scale).astype(bf16)


def gradient_first(core, hidden, in_all, solved, low_in, low_hid, before, token_count):
    tokens, columns = hidden.shape
    parts, rows, _ = in_all.shape
    rank = low_hid.shape[0]
    chunk, half = tokens // 2, columns // 2
    last = len(before) > 0
    block_spec = pl.BlockSpec((rows, half), lambda i: (0, 0))
    return pl.pallas_call(
        functools.partial(first_kernel, 1.0 / token_count if last else 1.0),
        out_shape=[
            jax.ShapeDtypeStruct((tokens, columns), bf16),
            jax.ShapeDtypeStruct((rows, half), bf16 if last else f32),
            jax.ShapeDtypeStruct((rows, half), bf16 if last else f32),
        ],
        grid=(2,),
        in_specs=[
            pl.BlockSpec((chunk, columns), lambda i: (i, 0)),
            pl.BlockSpec((parts, rows, chunk), lambda i: (0, 0, 2 * core + i)),
            pl.BlockSpec((chunk, 2 * rank), lambda i: (i, 0)),
            pl.BlockSpec((parts, rows, rank), lambda i: (0, 0, 0)),
            pl.BlockSpec((rank, columns), lambda i: (0, 0)),
        ]
        + [block_spec] * len(before),
        out_specs=[pl.BlockSpec((chunk, columns), lambda i: (i, 0)), block_spec, block_spec],
        scratch_shapes=[pltpu.VMEM((rows, half), f32)] * 2,
        compiler_params=pltpu.CompilerParams(vmem_limit_bytes=48 * 2**20),
        cost_estimate=pl.CostEstimate(
            flops=2_500_000_000, bytes_accessed=15_000_000, transcendentals=0
        ),
        name="gradient_first",
    )(hidden, in_all, solved, low_in, low_hid, *before)


def gradient_rest(offsets, blocks, hat_own, hat_other, in_all, solved_own, solved_other, low_in, token_count):
    tokens, columns = hat_own.shape
    parts, rows, _ = in_all.shape
    rank = low_in.shape[2]
    chunk, half = tokens // 2, columns // 2

    def first(i):
        return jnp.minimum(i, 1), 0

    def second(i):
        return jnp.maximum(i - 2, 0), 0

    return pl.pallas_call(
        functools.partial(rest_kernel, 1.0 / token_count, offsets),
        out_shape=[jax.ShapeDtypeStruct((blocks * rows, half), bf16)] * 2,
        grid=(4,),
        in_specs=[
            pl.BlockSpec((chunk, columns), first),
            pl.BlockSpec((chunk, columns), second),
            pl.BlockSpec((parts, rows, chunk), lambda i: (0, 0, i)),
            pl.BlockSpec((chunk, 2 * rank), first),
            pl.BlockSpec((chunk, 2 * rank), second),
            pl.BlockSpec((parts, rows, rank), lambda i: (0, 0, 0)),
        ],
        out_specs=[pl.BlockSpec((blocks * rows, half), lambda i: (0, 0))] * 2,
        scratch_shapes=[pltpu.VMEM((len(offsets) * rows, chunk), bf16)]
        + [pltpu.VMEM((blocks * rows, half), f32)] * 2,
        compiler_params=pltpu.CompilerParams(vmem_limit_bytes=48 * 2**20),
        cost_estimate=pl.CostEstimate(
            flops=2_500_000_000 * blocks, bytes_accessed=15_000_000, transcendentals=0
        ),
        name="gradient_rest",
    )(hat_own, hat_other, in_all, solved_own, solved_other, low_in)


def project_kernel(
    token_count, mine_ref, other_ref, omega_in_ref, omega_hid_ref, in_ref, hid_ref, both_ref, low_ref, blocks_ref, sketch_ref
):
    rank = sketch_ref.shape[0]
    me = lax.axis_index("c")
    sketch_ref[pl.ds(pl.multiple_of(me * (rank // 2), rank // 2), rank // 2), :] = mine_ref[...]
    sketch_ref[pl.ds(pl.multiple_of((1 - me) * (rank // 2), rank // 2), rank // 2), :] = other_ref[...]
    pieces = both_ref.shape[0]
    core_rows = 2 * rank // pieces
    tokens = in_ref.shape[0] // pieces
    start = 0
    for i, (omega, values) in enumerate(((omega_in_ref, in_ref), (omega_hid_ref, hid_ref))):
        end = start + values.shape[1]
        basis = sketch_ref[:, start:end]
        moment = jnp.dot(basis, omega[...], preferred_element_type=f32) / token_count
        square = row_product(basis, basis) / (float(token_count) * token_count)
        core = damping * 0.5 * (moment + moment.T) + square
        high = core.astype(bf16)
        rest = (core - high.astype(f32)).astype(bf16)
        low = (basis.astype(f32) / token_count).astype(bf16)
        if i == 0:
            turned = low.astype(f32).T.astype(bf16)
            block = blocks_ref.shape[1]
            for k in range(blocks_ref.shape[0]):
                blocks_ref[k] = turned[k * block : (k + 1) * block]
        else:
            low_ref[...] = low
        reach = row_product(values[...], low).astype(bf16)
        for k in range(pieces // 2):
            at = slice(k * core_rows, (k + 1) * core_rows)
            both_ref[i * pieces // 2 + k, :core_rows, :rank] = high[at]
            both_ref[i * pieces // 2 + k, :core_rows, rank:] = rest[at]
        for k in range(pieces):
            both_ref[k, core_rows:, i * rank : (i + 1) * rank] = reach[k * tokens : (k + 1) * tokens]
        start = end


def project(mine, other, omega_in, omega_hid, inputs, hidden_err, token_count):
    rank, width = 2 * mine.shape[0], mine.shape[1]
    tokens, local_in = inputs.shape
    rows = 2 * rank // N_MP + tokens // N_MP
    return pl.pallas_call(
        functools.partial(project_kernel, token_count),
        out_shape=[
            jax.ShapeDtypeStruct((N_MP, rows, 2 * rank), bf16),
            jax.ShapeDtypeStruct((rank, width - local_in), bf16),
            jax.ShapeDtypeStruct((4, local_in // 4, rank), bf16),
        ],
        in_specs=[pl.BlockSpec(memory_space=pltpu.VMEM)] * 6,
        out_specs=[pl.BlockSpec(memory_space=pltpu.VMEM)] * 3,
        scratch_shapes=[pltpu.VMEM((rank, width), bf16)],
        compiler_params=pltpu.CompilerParams(vmem_limit_bytes=24 * 2**20),
        name="project",
    )(mine, other, omega_in, omega_hid, inputs, hidden_err)


def two_halves(value):
    high = lax.reduce_precision(value, 8, 7)
    return jnp.concatenate([high.astype(bf16), (value - high).astype(bf16)], axis=-1)


def whole_value(halves):
    size = halves.shape[-1] // 2
    return halves[..., :size].astype(f32) + halves[..., size:].astype(f32)


def on_device(inputs, hidden_pre, hidden_grad, omega_in, omega_hid, owner_table):
    local_tokens, local_in = inputs.shape
    token_count = local_tokens * N_DP
    rank = omega_in.shape[1]
    block = local_in // 4
    near_tokens = 4 * local_tokens
    iy, ic, izh, izl = (lax.axis_index(a) for a in ("y", "c", "zh", "zl"))

    far = swap(inputs, "zl")

    hidden_err = (hidden_grad.astype(f32) * gelu_slope(hidden_pre)).astype(bf16)
    rows = jnp.concatenate(
        [
            jnp.dot(inputs, omega_in, preferred_element_type=f32).astype(bf16),
            jnp.dot(hidden_err, omega_hid, preferred_element_type=f32).astype(bf16),
        ],
        axis=1,
    )
    rows = after(rows.reshape(N_MP, local_tokens // N_MP, 2 * rank), far)
    rows = sum_scatter(rows, MP)
    near, far = (v.T.reshape(2, 2, block, local_tokens) for v in (inputs, far))
    for_y = []
    for k in range(4):
        to = (iy + k) % 4
        for_y.append(jnp.where(izl == to // 2, pick(near, to % 2), pick(far, to % 2)))
    in_parts = [for_y[0]] + [shift(for_y[k], "y", 4, k) for k in range(1, 4)]
    rows, in_parts[1], in_parts[3] = lax.optimization_barrier((rows, in_parts[1], in_parts[3]))
    rows = collect(rows, MP, N_MP).reshape(local_tokens, 2 * rank)
    rows, in_parts[2] = lax.optimization_barrier((rows, in_parts[2]))
    in_parts = jnp.stack(in_parts)
    in_parts = jnp.stack([pick(jnp.moveaxis(in_parts, 1, 0), ic), swap(pick(jnp.moveaxis(in_parts, 1, 0), 1 - ic), "c")])
    in_parts = [in_parts[:, k] for k in range(4)]

    sketch = jnp.concatenate(
        [
            token_product(rows[:, :rank], inputs).astype(bf16),
            token_product(rows[:, rank:], hidden_err).astype(bf16),
        ],
        axis=1,
    )
    in_near = line_up(in_parts, "y", 2)
    in_all = lax.all_gather(in_near, "x")

    width = sketch.shape[1]
    halves = sketch.reshape(2, rank // 2, width)
    part = pick(halves, ic).astype(f32) + swap(pick(halves, 1 - ic), "c").astype(f32)
    part = after(part.astype(bf16), in_near)
    part = sum_scatter(part.reshape(4, rank // 8, width), "y")
    part = sum_scatter(part.reshape(4, rank // 32, width), "zh")
    hid_own = lax.all_gather(hidden_err, "y").reshape(near_tokens, -1)
    part = collect(part, "zh", 4).reshape(rank // 8, width)
    part = collect(part, "y", 4).reshape(rank // 2, width)
    other = swap(part, "c")
    both, low_hid, low_blocks = project(
        part, other, omega_in, omega_hid, inputs, hidden_err, token_count
    )
    low_block = pick(low_blocks, (iy % 2) * 2 + ic)
    low_far = swap(low_block, "zl")
    both = exchange(after(both, in_all), MP)
    both, low_far = lax.optimization_barrier((both, low_far))
    low_block = jnp.where(izl == iy // 2, low_block, low_far)
    low_parts = [low_block] + [shift(low_block, "x", 4, k) for k in range(1, 4)]
    core_rows = 2 * rank // N_MP
    core = whole_value(both[:, :core_rows]).sum(0)
    reach = both[:, core_rows:].astype(f32).sum(0).astype(bf16)
    both = jnp.concatenate([two_halves(core), reach])
    both = collect(both, MP, N_MP)
    both, low_parts = lax.optimization_barrier((both, low_parts))
    reach = both[:, core_rows:].reshape(local_tokens, 2 * rank)

    reach_parts = [reach] + [shift(reach, "y", 4, k) for k in range(1, 4)]
    owner = owner_table[lax.axis_index(DP)]
    held, inverse = factor_and_inverse(owner, both, rank)
    inverse, reach_parts, hid_own = lax.optimization_barrier((inverse, reach_parts, hid_own))
    hid_other = swap(hid_own, "c")
    solved_own, low_in = solve(reach_parts, low_parts, inverse)
    solved_own = solved_own.reshape(near_tokens, 2 * rank)
    solved_other = swap(solved_own, "c")
    hat_own, up, down = gradient_first(
        0, hid_own, in_all, solved_own, low_in, low_hid, (), token_count
    )
    up, down, hid_other, solved_other = lax.optimization_barrier(
        (up, down, hid_other, solved_other)
    )
    hat_other, up, down = gradient_first(
        1, hid_other, in_all, solved_other, low_in, low_hid, (up, down), token_count
    )
    quarter = up.shape[1] // 2

    def pass_on(values, more_up, more_down, at):
        passed = []
        for k, value in enumerate(values):
            value = shift(value, "zh", 4, 1 if k < 2 else 3).astype(f32)
            here = (more_up if k < 2 else more_down)[at[k // 2] * block : (at[k // 2] + 1) * block]
            here = here[:, (k % 2) * quarter : (k % 2 + 1) * quarter]
            passed.append((value + here.astype(f32)).astype(bf16))
        return passed

    done = [v[:, k * quarter : (k + 1) * quarter] for v in (up, down) for k in range(2)]
    more = gradient_rest(
        (2,), 1, hat_own, hat_other, in_all, solved_own, solved_other, low_in, token_count
    )
    done = pass_on(done, *more, (0, 0))
    done, hat_own = lax.optimization_barrier((done, hat_own))
    more = gradient_rest(
        (1, 0, 3), 2, hat_own, hat_other, in_all, solved_own, solved_other, low_in, token_count
    )
    done = pass_on(done, *more, (0, 1))
    done = pass_on(done, *more, (1, 0))
    return (jnp.concatenate(done, axis=1), held)


def solution(mesh):
    parts = Mesh(
        mesh.devices.reshape([size for _, size in PARTS]), [name for name, _ in PARTS]
    )
    return jax.shard_map(
        on_device,
        mesh=parts,
        in_specs=(P(DP, MP), P(DP, MP), P(DP, MP), P(MP, None), P(MP, None), P()),
        out_specs=(P(DP, MP), P(DP, None, None)),
        check_vma=False,
    )
```

```python
import functools

import jax
import jax.numpy as jnp
from jax import lax
from jax.experimental import pallas as pl
from jax.experimental.pallas import tpu as pltpu
from jax.sharding import Mesh
from jax.sharding import PartitionSpec as P

damping = 0.25
half_root = 0.7071067811865476
inverse_root_tau = 0.3989422804014327

PARTS = (("zh", 4), ("y", 4), ("c", 2), ("x", 4), ("zl", 2))
DP = ("zh", "y", "c")
MP = ("x", "zl")
N_DP = 32
N_MP = 8
PANEL = 64
GROUP = 16
bf16 = jnp.bfloat16
f32 = jnp.float32


def gelu_slope(pre_values):
    values = pre_values.astype(f32)
    return (
        0.5 * (1.0 + lax.erf(values * half_root))
        + values * jnp.exp(-0.5 * values * values) * inverse_root_tau
    )


def token_product(left_side, right_side):
    return lax.dot_general(
        left_side, right_side, (((0,), (0,)), ((), ())), preferred_element_type=f32
    )


def row_product(left_side, right_side):
    return lax.dot_general(
        left_side, right_side, (((1,), (1,)), ((), ())), preferred_element_type=f32
    )


def exact_dot(left_side, right_side, dims):
    return lax.dot_general(
        left_side,
        right_side,
        (dims, ((), ())),
        precision=lax.Precision.HIGHEST,
        preferred_element_type=f32,
    )


def exchange(parts, axis):
    return lax.all_to_all(parts, axis, 0, 0)


def sum_scatter(parts, axis):
    return exchange(parts, axis).astype(f32).sum(0).astype(bf16)


def collect(part, axis, count):
    return exchange(jnp.broadcast_to(part[None], (count,) + part.shape), axis)


def shift(value, axis, count, step):
    return lax.ppermute(value, axis, [(i, (i + step) % count) for i in range(count)])


def swap(value, axis):
    return lax.ppermute(value, axis, [(0, 1), (1, 0)])


def pick(stack, index):
    return lax.dynamic_index_in_dim(stack, index, 0, False)


def after(value, *others):
    return lax.optimization_barrier((value,) + others)[0]


def line_up(parts, axis, pieces):
    count = len(parts)
    rows, columns = parts[0].shape[1:]
    if pieces == 1:
        shape = (count, rows, columns)
    else:
        shape = (rows, pieces * count * columns)

    def kernel(*refs):
        part_refs, out_ref, sems = refs[:count], refs[count], refs[count + 1]
        me = lax.axis_index(axis)
        copies = []
        for k in range(count):
            at = lax.rem(me - k + count, count)
            for piece in range(pieces):
                if pieces == 1:
                    target = out_ref.at[at]
                else:
                    start = pl.multiple_of((piece * count + at) * columns, columns)
                    target = out_ref.at[:, pl.ds(start, columns)]
                copies.append(
                    pltpu.make_async_copy(
                        part_refs[k].at[piece], target, sems.at[k * pieces + piece]
                    )
                )
        for copy in copies:
            copy.start()
        for copy in copies:
            copy.wait()

    return pl.pallas_call(
        kernel,
        out_shape=jax.ShapeDtypeStruct(shape, parts[0].dtype),
        in_specs=[pl.BlockSpec(memory_space=pl.ANY)] * count,
        out_specs=pl.BlockSpec(memory_space=pltpu.HBM),
        scratch_shapes=[pltpu.SemaphoreType.DMA((count * pieces,))],
        compiler_params=pltpu.CompilerParams(vmem_limit_bytes=2**20),
        name="line_up",
    )(*parts)


def eliminate(block):
    size = block.shape[0]
    rows = lax.broadcasted_iota(jnp.int32, (size, size), 0)
    lanes = lax.broadcasted_iota(jnp.int32, (size, size), 1)
    work = jnp.concatenate([block, (lanes == rows).astype(f32)], axis=1)
    row_ids = lax.broadcasted_iota(jnp.int32, (size, 2 * size), 0)
    inverse_pivots = []
    for first in range(0, size, GROUP):
        columns = [
            jnp.broadcast_to(work[:, first + k : first + k + 1], (size, 2 * size))
            for k in range(GROUP)
        ]
        heads = [work[first + k : first + k + 1, :] for k in range(GROUP)]
        for k in range(GROUP):
            at = first + k
            inverse = 1.0 / columns[k][at : at + 1, :]
            inverse_pivots.append(inverse)
            factor = jnp.where(row_ids > at, columns[k] * inverse, 0.0)
            work = work - factor * heads[k]
            for later in range(k + 1, GROUP):
                columns[later] = columns[later] - factor * columns[later][at : at + 1, :]
                heads[later] = (
                    heads[later] - factor[first + later : first + later + 1, :] * heads[k]
                )
    return (work * jnp.sqrt(jnp.concatenate(inverse_pivots, axis=0)))[:, size:]


def factor_kernel(owner_ref, both_ref, held_ref, inverse_ref, work):
    count, size, _ = inverse_ref.shape
    pieces = both_ref.shape[0] // count
    piece = size // pieces
    rows = lax.broadcasted_iota(jnp.int32, (size, size), 0)
    lanes = lax.broadcasted_iota(jnp.int32, (size, size), 1)
    for i in range(count):
        for k in range(pieces):
            halves = both_ref[i * pieces + k, :piece, :].astype(f32)
            work[i, k * piece : (k + 1) * piece, :size] = halves[:, :size] + halves[:, size:]
        work[i, :, size:] = (rows == lanes).astype(f32)
    for low in range(0, size, PANEL):
        high = low + PANEL
        panels = []
        for i in range(count):
            small = eliminate(work[i, low:high, low:high])
            panel = exact_dot(small, work[i, low:high, :], ((1,), (0,)))
            work[i, low:high, :] = panel
            panels.append(panel)
        if high < size:
            for i in range(count):
                work[i, high:, :] = work[i, high:, :] - exact_dot(
                    panels[i][:, high:size], panels[i], ((0,), (0,))
                )
    for i in range(count):
        @pl.when(owner_ref[0] == i)
        def _(i=i):
            held_ref[0] = jnp.where(rows <= lanes, work[i, :, :size], 0.0).T

        inverse_ref[i] = exact_dot(work[i, :, size:], work[i, :, size:], ((0,), (0,)))


def factor_and_inverse(owner, both, size):
    return pl.pallas_call(
        factor_kernel,
        out_shape=[
            jax.ShapeDtypeStruct((1, size, size), f32),
            jax.ShapeDtypeStruct((2, size, size), f32),
        ],
        in_specs=[
            pl.BlockSpec(memory_space=pltpu.SMEM),
            pl.BlockSpec(memory_space=pltpu.VMEM),
        ],
        out_specs=[pl.BlockSpec(memory_space=pltpu.VMEM)] * 2,
        scratch_shapes=[pltpu.VMEM((2, size, 2 * size), f32)],
        compiler_params=pltpu.CompilerParams(vmem_limit_bytes=16 * 2**20),
        cost_estimate=pl.CostEstimate(
            flops=12 * size**3, bytes_accessed=60_000_000, transcendentals=0
        ),
        name="factor_and_inverse",
    )(owner, both)


def solve_kernel(*refs):
    reach_refs, low_refs, inverse_ref, out_ref, low_ref = refs[:4], refs[4:8], *refs[8:]
    size = inverse_ref.shape[1]
    iy, ix = lax.axis_index("y"), lax.axis_index("x")
    inverses = []
    for i in range(2):
        rest, pieces = inverse_ref[i], []
        for _ in range(3):
            pieces.append(rest.astype(bf16))
            rest = rest - pieces[-1].astype(f32)
        inverses.append(pieces)
    for k in range(4):
        low_ref[lax.rem(ix - k + 4, 4)] = low_refs[k][...]
        at = lax.rem(iy - k + 4, 4)
        for i in range(2):
            reach = reach_refs[k][:, i * size : (i + 1) * size]
            solved = sum(
                jnp.dot(reach, piece, preferred_element_type=f32) for piece in inverses[i][::-1]
            )
            out_ref[at, :, i * size : (i + 1) * size] = solved.astype(bf16)


def solve(reach_parts, low_parts, inverse):
    return pl.pallas_call(
        solve_kernel,
        out_shape=[
            jax.ShapeDtypeStruct((4,) + reach_parts[0].shape, bf16),
            jax.ShapeDtypeStruct((4,) + low_parts[0].shape, bf16),
        ],
        in_specs=[pl.BlockSpec(memory_space=pltpu.VMEM)] * 9,
        out_specs=[pl.BlockSpec(memory_space=pltpu.VMEM)] * 2,
        compiler_params=pltpu.CompilerParams(vmem_limit_bytes=16 * 2**20),
        name="solve",
    )(*reach_parts, *low_parts, inverse)


def removed(values, taken):
    return ((values.astype(f32) - taken) * (1.0 / damping)).astype(bf16)


def add_term(total, term, step):
    @pl.when(step == 0)
    def _():
        total[...] = term

    @pl.when(step > 0)
    def _():
        total[...] = total[...] + term


def first_kernel(scale, hidden_ref, in_ref, solved_ref, low_in_ref, low_hid_ref, *refs):
    before, (hat_ref, up_ref, down_ref, up_total, down_total) = refs[:-5], refs[-5:]
    step, steps = pl.program_id(0), pl.num_programs(0)
    me = lax.axis_index("zh")
    rank, columns = low_hid_ref.shape
    taken = jnp.dot(solved_ref[:, rank:], low_hid_ref[...], preferred_element_type=f32)
    hat_hid = removed(hidden_ref[...], taken)
    hat_ref[...] = hat_hid
    for total, off, start in ((up_total, 3, 0), (down_total, 1, columns // 2)):
        at = lax.rem(me + off, 4)
        hat_in = removed(in_ref[at], row_product(low_in_ref[at], solved_ref[:, :rank]))
        part = hat_hid[:, start : start + columns // 2]
        add_term(total, jnp.dot(hat_in, part, preferred_element_type=f32), step)

    @pl.when(step == steps - 1)
    def _():
        up, down = up_total[...], down_total[...]
        if before:
            up, down = up + before[0][...], down + before[1][...]
        up_ref[...] = (up * scale).astype(up_ref.dtype)
        down_ref[...] = (down * scale).astype(down_ref.dtype)


def rest_kernel(
    scale, hat_own_ref, hat_other_ref, in_ref, solved_own_ref, solved_other_ref, low_in_ref, up_ref, down_ref, hat_in, up_total, down_total
):
    step, steps = pl.program_id(0), pl.num_programs(0)
    me = lax.axis_index("zh")
    rank, columns = low_in_ref.shape[2], hat_own_ref.shape[1]
    rows = in_ref.shape[1]

    def body(hat_ref, solved_ref):
        for k, off in enumerate((1, 0, 2, 3)):
            at = lax.rem(me + off, 4)
            taken = row_product(low_in_ref[at], solved_ref[:, :rank])
            hat_in[k * rows : (k + 1) * rows, :] = removed(in_ref[at], taken)
        for total, low, start in ((up_total, 0, 0), (down_total, rows, columns // 2)):
            term = jnp.dot(
                hat_in[low : low + 3 * rows, :],
                hat_ref[:, start : start + columns // 2],
                preferred_element_type=f32,
            )
            add_term(total, term, step)

    pl.when(step < steps // 2)(functools.partial(body, hat_own_ref, solved_own_ref))
    pl.when(step >= steps // 2)(functools.partial(body, hat_other_ref, solved_other_ref))

    @pl.when(step == steps - 1)
    def _():
        up_ref[...] = (up_total[...] * scale).astype(bf16)
        down_ref[...] = (down_total[...] * scale).astype(bf16)


def gradient_first(core, hidden, in_all, solved, low_in, low_hid, before, token_count):
    tokens, columns = hidden.shape
    parts, rows, _ = in_all.shape
    rank = low_hid.shape[0]
    chunk, half = tokens // 2, columns // 2
    last = len(before) > 0
    block_spec = pl.BlockSpec((rows, half), lambda i: (0, 0))
    return pl.pallas_call(
        functools.partial(first_kernel, 1.0 / token_count if last else 1.0),
        out_shape=[
            jax.ShapeDtypeStruct((tokens, columns), bf16),
            jax.ShapeDtypeStruct((rows, half), bf16 if last else f32),
            jax.ShapeDtypeStruct((rows, half), bf16 if last else f32),
        ],
        grid=(2,),
        in_specs=[
            pl.BlockSpec((chunk, columns), lambda i: (i, 0)),
            pl.BlockSpec((parts, rows, chunk), lambda i: (0, 0, 2 * core + i)),
            pl.BlockSpec((chunk, 2 * rank), lambda i: (i, 0)),
            pl.BlockSpec((parts, rows, rank), lambda i: (0, 0, 0)),
            pl.BlockSpec((rank, columns), lambda i: (0, 0)),
        ]
        + [block_spec] * len(before),
        out_specs=[pl.BlockSpec((chunk, columns), lambda i: (i, 0)), block_spec, block_spec],
        scratch_shapes=[pltpu.VMEM((rows, half), f32)] * 2,
        compiler_params=pltpu.CompilerParams(vmem_limit_bytes=48 * 2**20),
        cost_estimate=pl.CostEstimate(
            flops=2_500_000_000, bytes_accessed=15_000_000, transcendentals=0
        ),
        name="gradient_first",
    )(hidden, in_all, solved, low_in, low_hid, *before)


def gradient_rest(hat_own, hat_other, in_all, solved_own, solved_other, low_in, token_count):
    tokens, columns = hat_own.shape
    parts, rows, _ = in_all.shape
    rank = low_in.shape[2]
    chunk, half = tokens // 2, columns // 2

    def first(i):
        return jnp.minimum(i, 1), 0

    def second(i):
        return jnp.maximum(i - 2, 0), 0

    return pl.pallas_call(
        functools.partial(rest_kernel, 1.0 / token_count),
        out_shape=[jax.ShapeDtypeStruct((3 * rows, half), bf16)] * 2,
        grid=(4,),
        in_specs=[
            pl.BlockSpec((chunk, columns), first),
            pl.BlockSpec((chunk, columns), second),
            pl.BlockSpec((parts, rows, chunk), lambda i: (0, 0, i)),
            pl.BlockSpec((chunk, 2 * rank), first),
            pl.BlockSpec((chunk, 2 * rank), second),
            pl.BlockSpec((parts, rows, rank), lambda i: (0, 0, 0)),
        ],
        out_specs=[pl.BlockSpec((3 * rows, half), lambda i: (0, 0))] * 2,
        scratch_shapes=[pltpu.VMEM((4 * rows, chunk), bf16)]
        + [pltpu.VMEM((3 * rows, half), f32)] * 2,
        compiler_params=pltpu.CompilerParams(vmem_limit_bytes=48 * 2**20),
        cost_estimate=pl.CostEstimate(
            flops=7_000_000_000, bytes_accessed=20_000_000, transcendentals=0
        ),
        name="gradient_rest",
    )(hat_own, hat_other, in_all, solved_own, solved_other, low_in)


def project_kernel(
    token_count, mine_ref, other_ref, omega_in_ref, omega_hid_ref, in_ref, hid_ref, both_ref, low_ref, blocks_ref, sketch_ref
):
    rank = sketch_ref.shape[0]
    me = lax.axis_index("c")
    sketch_ref[pl.ds(pl.multiple_of(me * (rank // 2), rank // 2), rank // 2), :] = mine_ref[...]
    sketch_ref[pl.ds(pl.multiple_of((1 - me) * (rank // 2), rank // 2), rank // 2), :] = other_ref[...]
    pieces = both_ref.shape[0]
    core_rows = 2 * rank // pieces
    tokens = in_ref.shape[0] // pieces
    start = 0
    for i, (omega, values) in enumerate(((omega_in_ref, in_ref), (omega_hid_ref, hid_ref))):
        end = start + values.shape[1]
        basis = sketch_ref[:, start:end]
        moment = jnp.dot(basis, omega[...], preferred_element_type=f32) / token_count
        square = row_product(basis, basis) / (float(token_count) * token_count)
        core = damping * 0.5 * (moment + moment.T) + square
        high = core.astype(bf16)
        rest = (core - high.astype(f32)).astype(bf16)
        low = (basis.astype(f32) / token_count).astype(bf16)
        if i == 0:
            turned = low.astype(f32).T.astype(bf16)
            block = blocks_ref.shape[1]
            for k in range(blocks_ref.shape[0]):
                blocks_ref[k] = turned[k * block : (k + 1) * block]
        else:
            low_ref[...] = low
        reach = row_product(values[...], low).astype(bf16)
        for k in range(pieces // 2):
            at = slice(k * core_rows, (k + 1) * core_rows)
            both_ref[i * pieces // 2 + k, :core_rows, :rank] = high[at]
            both_ref[i * pieces // 2 + k, :core_rows, rank:] = rest[at]
        for k in range(pieces):
            both_ref[k, core_rows:, i * rank : (i + 1) * rank] = reach[k * tokens : (k + 1) * tokens]
        start = end


def project(mine, other, omega_in, omega_hid, inputs, hidden_err, token_count):
    rank, width = 2 * mine.shape[0], mine.shape[1]
    tokens, local_in = inputs.shape
    rows = 2 * rank // N_MP + tokens // N_MP
    return pl.pallas_call(
        functools.partial(project_kernel, token_count),
        out_shape=[
            jax.ShapeDtypeStruct((N_MP, rows, 2 * rank), bf16),
            jax.ShapeDtypeStruct((rank, width - local_in), bf16),
            jax.ShapeDtypeStruct((4, local_in // 4, rank), bf16),
        ],
        in_specs=[pl.BlockSpec(memory_space=pltpu.VMEM)] * 6,
        out_specs=[pl.BlockSpec(memory_space=pltpu.VMEM)] * 3,
        scratch_shapes=[pltpu.VMEM((rank, width), bf16)],
        compiler_params=pltpu.CompilerParams(vmem_limit_bytes=24 * 2**20),
        name="project",
    )(mine, other, omega_in, omega_hid, inputs, hidden_err)


def two_halves(value):
    high = lax.reduce_precision(value, 8, 7)
    return jnp.concatenate([high.astype(bf16), (value - high).astype(bf16)], axis=-1)


def whole_value(halves):
    size = halves.shape[-1] // 2
    return halves[..., :size].astype(f32) + halves[..., size:].astype(f32)


def on_device(inputs, hidden_pre, hidden_grad, omega_in, omega_hid, owner_table):
    local_tokens, local_in = inputs.shape
    token_count = local_tokens * N_DP
    rank = omega_in.shape[1]
    block = local_in // 4
    near_tokens = 4 * local_tokens
    iy, ic, izh, izl = (lax.axis_index(a) for a in ("y", "c", "zh", "zl"))

    far = swap(inputs, "zl")

    hidden_err = (hidden_grad.astype(f32) * gelu_slope(hidden_pre)).astype(bf16)
    rows = jnp.concatenate(
        [
            jnp.dot(inputs, omega_in, preferred_element_type=f32).astype(bf16),
            jnp.dot(hidden_err, omega_hid, preferred_element_type=f32).astype(bf16),
        ],
        axis=1,
    )
    rows = after(rows.reshape(N_MP, local_tokens // N_MP, 2 * rank), far)
    rows = sum_scatter(rows, MP)
    near, far = (v.T.reshape(2, 2, block, local_tokens) for v in (inputs, far))
    for_y = []
    for k in range(4):
        to = (iy + k) % 4
        for_y.append(jnp.where(izl == to // 2, pick(near, to % 2), pick(far, to % 2)))
    in_parts = [for_y[0]] + [shift(for_y[k], "y", 4, k) for k in range(1, 4)]
    rows, in_parts[1], in_parts[3] = lax.optimization_barrier((rows, in_parts[1], in_parts[3]))
    rows = collect(rows, MP, N_MP).reshape(local_tokens, 2 * rank)
    rows, in_parts[2] = lax.optimization_barrier((rows, in_parts[2]))
    in_parts = jnp.stack(in_parts)
    in_parts = jnp.stack([pick(jnp.moveaxis(in_parts, 1, 0), ic), swap(pick(jnp.moveaxis(in_parts, 1, 0), 1 - ic), "c")])
    in_parts = [in_parts[:, k] for k in range(4)]

    sketch = jnp.concatenate(
        [
            token_product(rows[:, :rank], inputs).astype(bf16),
            token_product(rows[:, rank:], hidden_err).astype(bf16),
        ],
        axis=1,
    )
    in_near = line_up(in_parts, "y", 2)
    in_all = lax.all_gather(in_near, "x")

    width = sketch.shape[1]
    halves = sketch.reshape(2, rank // 2, width)
    part = pick(halves, ic).astype(f32) + swap(pick(halves, 1 - ic), "c").astype(f32)
    part = after(part.astype(bf16), in_near)
    part = sum_scatter(part.reshape(4, rank // 8, width), "y")
    part = sum_scatter(part.reshape(4, rank // 32, width), "zh")
    hid_own = lax.all_gather(hidden_err, "y").reshape(near_tokens, -1)
    part = collect(part, "zh", 4).reshape(rank // 8, width)
    part = collect(part, "y", 4).reshape(rank // 2, width)
    other = swap(part, "c")
    both, low_hid, low_blocks = project(
        part, other, omega_in, omega_hid, inputs, hidden_err, token_count
    )
    low_block = pick(low_blocks, (iy % 2) * 2 + ic)
    low_far = swap(low_block, "zl")
    both = exchange(after(both, in_all), MP)
    both, low_far = lax.optimization_barrier((both, low_far))
    low_block = jnp.where(izl == iy // 2, low_block, low_far)
    low_parts = [low_block] + [shift(low_block, "x", 4, k) for k in range(1, 4)]
    core_rows = 2 * rank // N_MP
    core = whole_value(both[:, :core_rows]).sum(0)
    reach = both[:, core_rows:].astype(f32).sum(0).astype(bf16)
    both = jnp.concatenate([two_halves(core), reach])
    both = collect(both, MP, N_MP)
    both, low_parts = lax.optimization_barrier((both, low_parts))
    reach = both[:, core_rows:].reshape(local_tokens, 2 * rank)

    reach_parts = [reach] + [shift(reach, "y", 4, k) for k in range(1, 4)]
    owner = owner_table[lax.axis_index(DP)]
    held, inverse = factor_and_inverse(owner, both, rank)
    inverse, reach_parts, hid_own = lax.optimization_barrier((inverse, reach_parts, hid_own))
    hid_other = swap(hid_own, "c")
    solved_own, low_in = solve(reach_parts, low_parts, inverse)
    solved_own = solved_own.reshape(near_tokens, 2 * rank)
    solved_other = swap(solved_own, "c")
    hat_own, up, down = gradient_first(
        0, hid_own, in_all, solved_own, low_in, low_hid, (), token_count
    )
    up, down, hid_other, solved_other = lax.optimization_barrier(
        (up, down, hid_other, solved_other)
    )
    hat_other, up, down = gradient_first(
        1, hid_other, in_all, solved_other, low_in, low_hid, (up, down), token_count
    )
    more_up, more_down = gradient_rest(
        hat_own, hat_other, in_all, solved_own, solved_other, low_in, token_count
    )
    done = []
    for running, more, turn, order in ((up, more_up, 1, (2, 0, 1)), (down, more_down, 3, (1, 2, 0))):
        for at in order:
            running = shift(running, "zh", 4, turn).astype(f32)
            here = more[at * block : (at + 1) * block].astype(f32)
            running = (running + here).astype(bf16)
        done.append(running)
    return (jnp.concatenate(done, axis=1), held)


def solution(mesh):
    parts = Mesh(
        mesh.devices.reshape([size for _, size in PARTS]), [name for name, _ in PARTS]
    )
    return jax.shard_map(
        on_device,
        mesh=parts,
        in_specs=(P(DP, MP), P(DP, MP), P(DP, MP), P(MP, None), P(MP, None), P()),
        out_specs=(P(DP, MP), P(DP, None, None)),
        check_vma=False,
    )
```
